1024 devices in a mesh: grp: 16 (over z, core), rep: 64 (over x, y).
Axes of the slice: x: 8, y: 8, z: 8, core: 2. Of those that a mesh axis runs over, the one named last changes fastest.
Arguments:
- features: bfloat16 [131072, 512], P(('grp', 'rep'))
- output_grads: bfloat16 [131072, 8192], P(('grp', 'rep'))
- block_order: int32 [16], replicated, may hold values from 0 to 15, each once
- emb_table: float32 [524288, 128], P(('grp', 'rep')), may hold values from -6 to 6
- row_accum: float32 [524288], P(('grp', 'rep')), may hold values from 0.1 to 1
- hot_rows: int32 [131072], P(('grp', 'rep')), may hold values from 0 to 511
- hot_owner: int32 [131072, 1], P(('grp', 'rep')), may hold values from 0 to 15; in each aligned block of 128 rows (0 to 127, 128 to 255, ...) at most 16 rows name the same one
- live_counts: int32 [1024], P(('grp', 'rep')), may hold values from 32 to 128, as said below
- hot_deltas: bfloat16 [131072, 128], P(('grp', 'rep')), may hold values from -6 to 6
Outputs:
- new_table: float32 [524288, 128], P(('grp', 'rep'))
- new_accum: float32 [524288], P(('grp', 'rep'))
- directions: bfloat16 [16, 512, 512], P(None, 'rep')
The draws below stay inside these ranges and needn't reach their ends.
Inputs may be any that keep to these rules, and one draw needn't show every extreme that they name: `block_order`: A permutation: each block is taken by one owner. `hot_owner`: in the 128 slots of one device at most 16 name the same owner. `live_counts`: the live slots of a device are its first ones. `hot_rows`: A row among the owner's 512 rows.
All inputs are finite; a program needn't handle non-finite values.
Results may differ from the reference program's by a relative error of at most 0.001.
Values may be sent and summed in bfloat16 or wider, within the bound.
No kernel may reach another device: no remote copies, remote signals or barrier semaphores. Data moves between devices by JAX's collectives and lax.ppermute only.
A program may use at most 32 MiB of HBM per device.

```python
import math
import jax
import jax.numpy as jnp
import numpy as np
from jax import lax

B = 512
EMB = 128
ROWS_DEV = 512
HOT = 128
ITERS = 2
CAP = 16
NBLK = 16
TOKENS = 131072
ROWS = 524288
HOTS = 131072
N_GRP = 16
N_REP = 64
DEVICES = 1024


def scaled_field(key, shape, columns, spread):
    key_scale, key_base = jax.random.split(key)
    scales = jnp.exp(jax.random.uniform(key_scale, (columns,), jnp.float32, 0.0, math.log(spread)))
    base = jax.random.normal(key_base, shape, jnp.float32)
    return base * scales[None, :] / math.sqrt(spread)


def draw_features(key, part):
    key = jax.random.fold_in(key, 3)
    return scaled_field(key, (TOKENS, B), B, 10.0).astype(jnp.bfloat16)


def draw_output_grads(key, part):
    key = jax.random.fold_in(key, 5)
    return scaled_field(key, (TOKENS, NBLK * B), NBLK * B, 30.0).astype(jnp.bfloat16)


def draw_live_counts(key, part):
    key = jax.random.fold_in(key, 7)
    key_count, key_order = jax.random.split(key)
    counts = jax.random.randint(key_count, (DEVICES,), HOT // 4, HOT + 1).astype(jnp.int32)
    order = jax.random.permutation(key_order, DEVICES)
    counts = counts.at[order[0]].set(HOT)
    counts = counts.at[order[1]].set(HOT // 4)
    return counts


def place_ends(values, rng, least, high):
    longest = values.shape.index(max(values.shape))
    spots = []
    for shift in (0, 1):
        where = [jax.random.randint(jax.random.fold_in(rng, axis), (), 0, length) for axis, length in enumerate(values.shape)]
        where[longest] = (where[longest] + shift) % values.shape[longest]
        spots.append(tuple(where))
    return values.at[spots[0]].set(least).at[spots[1]].set(high)


def block_scale(rng, extent, shards, low, largest):
    factor_of, own = 1.0, jax.random.fold_in(rng, 6)
    for position, blocks in shards:
        draws = jnp.exp(jax.random.uniform(jax.random.fold_in(own, position), (blocks,), jnp.float32, low / len(shards), largest / len(shards)))
        factor_of = factor_of * jnp.repeat(draws, extent[position] // blocks).reshape([-1 if axis == position else 1 for axis in range(len(extent))])
    return factor_of


def rank_bounds(amount, lean):
    weights = [(1 << 20) // math.isqrt(grade ** lean) + 1 for grade in range(1, amount + 1)]
    scale = 1 + sum(weights) // (1 << 30)
    return np.cumsum(np.array([max(1, weight // scale) for weight in weights]))


def ranked(own_key, extent, amount, skew):
    table = rank_bounds(amount, skew)
    pick = jax.random.randint(jax.random.fold_in(own_key, 1), extent, 0, int(table[amount - 1]))
    rank = jnp.searchsorted(jnp.asarray(table, jnp.int32), pick, side="right")
    return jax.random.permutation(jax.random.fold_in(own_key, 2), amount)[rank].astype(jnp.int32)


def assign_block(rng, own, number, rows, number_of, top, reach, lean):
    sequence = jax.random.permutation(rng, number_of)
    heavy_load, usual = shares(number_of, rows * top, reach, lean, True), shares(number_of, rows * top, reach, lean, False)
    places = jnp.arange(number_of)

    def named(tallies, turn):
        used = int((tallies > 0).sum())
        fixed = max(1, used // 4)
        shifted = fixed + (places - fixed + turn * (used - fixed)) % max(1, number_of - fixed)
        return jnp.zeros((number_of,), jnp.int32).at[sequence[jnp.where(places < fixed, places, shifted)]].set(jnp.asarray(tallies, jnp.int32))

    tallies = jnp.where(number % 4 == 0, named(heavy_load, number // 4), named(usual, number - number // 4 - 1))
    mixed = jax.random.permutation(jax.random.fold_in(own, 3), number_of)
    source_of, sink = mixed[0:number_of // 2 * 2:2], mixed[1:number_of // 2 * 2:2]
    slack = jnp.minimum(tallies[source_of] - 1, reach - tallies[sink]) // 2
    slack = jnp.where((source_of == sequence[0]) | (sink == sequence[0]) | (tallies[sink] == 0), 0, jnp.maximum(slack, 0))
    shifted = jax.random.randint(jax.random.fold_in(own, 4), (number_of // 2,), 0, 1 << 20) % (slack + 1)
    tallies = tallies.at[source_of].add(-shifted).at[sink].add(shifted)
    members = jnp.searchsorted(jnp.cumsum(tallies), jnp.arange(rows * top), side="right").astype(jnp.int32)
    listing = members.reshape(top, rows).T
    listing = listing[jax.random.permutation(jax.random.fold_in(own, 1), rows)]
    turn = jax.random.randint(jax.random.fold_in(own, 2), (rows, 1), 0, top)
    return jnp.take_along_axis(listing, (jnp.arange(top)[None, :] + turn) % top, axis=1)


def shares(count, total, most, skew, full):
    loads = [(1 << 20) // math.isqrt(rank ** skew) + 1 for rank in range(1, count + 1)]
    largest = most if full else min(most, max(-(-total // count), total * loads[0] // sum(loads)))
    least = 1 if total - largest >= count - 1 else 0
    given, rest = [largest] + [least] * (count - 1), total - largest - least * (count - 1)
    while rest > 0:
        movable = [i for i in range(1, count) if given[i] < largest] or [i for i in range(1, count) if given[i] < most]
        mass, remaining = sum([loads[i] for i in movable]), rest
        for i in movable:
            addition = min(most - given[i], max(1, remaining * loads[i] // mass), rest)
            given[i] = given[i] + addition
            rest = rest - addition
    return np.array(given)


def bell_draw(key, dims, scale, reach, cuts=(), kind=jnp.bfloat16):
    loudness = block_scale(key, dims, cuts, -0.22, 0.18) if cuts else 1.0
    drawn = jax.random.normal(key, dims, jnp.float32) * scale * loudness
    return jnp.minimum(jnp.maximum(drawn, -reach), reach).astype(kind)


def setup_inputs(seed: int = 0) -> dict:
    splits = jax.random.split(jax.random.key(seed), 10)
    features = draw_features(jax.random.fold_in(splits[9], 71), 0)
    output_grads = draw_output_grads(jax.random.fold_in(splits[9], 71), 0)
    block_order = jax.random.permutation(splits[2], NBLK).astype(jnp.int32)
    emb_table = bell_draw(splits[3], (ROWS, EMB), 1.0, 6.0, ((0, 1024),), jnp.float32)
    row_accum = jnp.clip(jnp.exp(math.log(1.0) - 2.3025851 * jax.random.uniform(splits[4], (ROWS,), jnp.float32) ** block_scale(splits[4], (ROWS,), ((0, 1024),), -0.2, 0.2)), 0.1, 1.0)
    hot_rows = place_ends(ranked(splits[5], (HOTS,), ROWS_DEV, 2), jax.random.fold_in(splits[5], 3), 0, ROWS_DEV - 1).astype(jnp.int32)
    hot_owner_keys = jax.random.split(jax.random.fold_in(splits[6], 1), HOTS // HOT)
    hot_owner_turns = jax.random.permutation(jax.random.fold_in(splits[6], 3), HOTS // HOT)
    hot_owner = jax.vmap(lambda own, number: assign_block(jax.random.fold_in(splits[6], 2), own, number, HOT, N_GRP, 1, CAP, 2))(hot_owner_keys, hot_owner_turns).reshape((HOTS, 1))
    live_counts = draw_live_counts(jax.random.fold_in(splits[9], 71), 0)
    hot_deltas = bell_draw(splits[8], (HOTS, EMB), 1.0, 6.0, ((0, 1024),))
    return {"features": features, "output_grads": output_grads, "block_order": block_order, "emb_table": emb_table, "row_accum": row_accum, "hot_rows": hot_rows, "hot_owner": hot_owner, "live_counts": live_counts, "hot_deltas": hot_deltas}


highest = lax.Precision.HIGHEST
learning_rate = 1.0

def inverse_root(statistic, scale):
    identity = jnp.eye(statistic.shape[0], dtype=jnp.float32)
    current = statistic / scale
    product = identity * scale ** (-0.25)
    for level in range(ITERS):
        factor = (5.0 * identity - current) / 4.0
        product = jnp.dot(product, factor, precision=highest)
        if level + 1 < ITERS:
            square = jnp.dot(factor, factor, precision=highest)
            fourth = jnp.dot(square, square, precision=highest)
            current = jnp.dot(fourth, current, precision=highest)
    return product

def reference(features, output_grads, block_order, emb_table, row_accum, hot_rows, hot_owner, live_counts, hot_deltas):
    slots = jnp.arange(HOTS).astype(jnp.int32)
    sender = (slots // HOT).astype(jnp.int32)
    within = (slots % HOT).astype(jnp.int32)
    owner_dev = hot_owner[:, 0].astype(jnp.int32) * N_REP + sender % N_REP
    global_row = (owner_dev * ROWS_DEV + hot_rows).astype(jnp.int32)
    live = within < live_counts[sender]
    masked = jnp.where(live[:, None], hot_deltas.astype(jnp.float32), jnp.zeros((HOTS, EMB), jnp.float32))
    summed = jnp.zeros((ROWS, EMB), jnp.float32).at[global_row].add(masked)
    new_accum = row_accum + lax.optimization_barrier(jnp.mean(summed * summed, axis=1))
    new_table = emb_table - learning_rate * summed / jnp.sqrt(new_accum)[:, None]

    def one_block(owner_slot):
        first = (block_order[owner_slot] * B).astype(jnp.int32)
        columns = lax.dynamic_slice_in_dim(output_grads, first, B, 1)
        grad = jnp.dot(features.T, columns, preferred_element_type=jnp.float32)
        frobenius = jnp.sum(grad * grad) + 1e-06
        normal_gram = jnp.dot(grad, grad.T, precision=highest) / frobenius
        squared_gram = jnp.dot(normal_gram, normal_gram, precision=highest)
        spectral_bound = jnp.sqrt(jnp.sqrt(jnp.sum(squared_gram * squared_gram)))
        scale = frobenius * spectral_bound
        left = inverse_root(jnp.dot(grad, grad.T, precision=highest), scale)
        right = inverse_root(jnp.dot(grad.T, grad, precision=highest), scale)
        result = B * jnp.dot(jnp.dot(left, grad, precision=highest), right, precision=highest)
        return result.astype(jnp.bfloat16)
    directions = lax.map(one_block, jnp.arange(NBLK).astype(jnp.int32))
    return (new_table, new_accum, directions)
```

```python
from functools import partial

import jax
import jax.numpy as jnp
from jax import lax
from jax.experimental import pallas as pl
from jax.experimental.pallas import tpu as pltpu
from jax.sharding import PartitionSpec as P

SIDE = 8
AXES = ("grp", "rep")
MIB = 1 << 20


def device(x, y, z, core):
    return ((z % SIDE) * 2 + core) * (SIDE * SIDE) + (x % SIDE) * SIDE + y % SIDE


def chips():
    for x in range(SIDE):
        for y in range(SIDE):
            for z in range(SIDE):
                yield x, y, z


def parity(x, y, z):
    return (y % 2) * 4 + (z % 2) * 2 + x % 2


def cube_groups():
    groups = []
    for core in range(2):
        for x, y, z in chips():
            if x % 2 != core or y % 2 != core or z % 2 != core:
                continue
            members = [None] * 8
            for dx in range(2):
                for dy in range(2):
                    for dz in range(2):
                        spot = ((x + dx) % SIDE, (y + dy) % SIDE, (z + dz) % SIDE)
                        members[parity(*spot)] = device(*spot, core)
            groups.append(members)
    return groups


def piece(x, y, z):
    return (((x // 2) * 4 + y // 2) * 2) + (z // 2) % 2


def stride_groups(split):
    groups = {}
    for core in range(2):
        for x, y, z in chips():
            half = z // 4
            key = (core, parity(x, y, z)) + ((half,) if split else ())
            order = piece(x, y, z) + (0 if split else 32 * half)
            groups.setdefault(key, []).append((order, device(x, y, z, core)))
    return [[d for _, d in sorted(members)] for members in groups.values()]


def core_pairs():
    return [(device(x, y, z, c), device(x, y, z, 1 - c)) for x, y, z in chips() for c in range(2)]


def home_pairs():
    pairs = []
    for x, y, z in chips():
        for core in range(2):
            to_x = (x & 4) | (core << 1) | ((x >> 1) & 1)
            to_y = (y & 6) | ((z >> 1) & 1)
            to_z = (z & 5) | ((y & 1) << 1)
            pairs.append((device(x, y, z, core), device(to_x, to_y, to_z, x & 1)))
    return pairs


def tokens_kernel(order, grads, features, out, sems):
    copies = []
    for spot in range(8):
        for k in range(2):
            first = pl.multiple_of(order[spot + 8 * k] * 512, 512)
            copies.append((grads.at[:, pl.ds(first, 512)], out.at[spot, k]))
        copies.append((features, out.at[spot, 2]))
    started = []
    for n, (source, target) in enumerate(copies):
        copy = pltpu.make_async_copy(source, target, sems.at[n])
        copy.start()
        started.append(copy)
    for copy in started:
        copy.wait()


def pack_tokens(order, grads, features):
    return pl.pallas_call(
        tokens_kernel,
        out_shape=jax.ShapeDtypeStruct((8, 3, 128, 512), jnp.bfloat16),
        in_specs=[
            pl.BlockSpec(memory_space=pltpu.SMEM),
            pl.BlockSpec(memory_space=pl.ANY),
            pl.BlockSpec(memory_space=pl.ANY),
        ],
        out_specs=pl.BlockSpec(memory_space=pl.ANY),
        scratch_shapes=[pltpu.SemaphoreType.DMA((24,))],
    )(order, grads, features)


def slots_kernel(live, rows, owner_col, owner_row, deltas, out):
    count = deltas.shape[0]
    before = lax.broadcasted_iota(jnp.int32, (count, count), 0)
    after = lax.broadcasted_iota(jnp.int32, (count, count), 1)
    same = (owner_col[...] == owner_row[...]) & (before < after)
    rank = jnp.sum(same.astype(jnp.float32), axis=0, keepdims=True)
    position = owner_row[...].astype(jnp.float32) * 16.0 + rank
    place = lax.broadcasted_iota(jnp.int32, (256, count), 0).astype(jnp.float32) == position
    place = place.astype(jnp.float32).astype(jnp.bfloat16)
    masked = jnp.where(before < live[0], deltas[...].astype(jnp.float32), 0.0).astype(jnp.bfloat16)
    high, low = rows[...] // 16, rows[...] % 16
    keys = jnp.where(after < 64, high, low).astype(jnp.float32).astype(jnp.bfloat16)
    moved = jnp.dot(place, masked, preferred_element_type=jnp.float32).astype(jnp.bfloat16)
    named = jnp.dot(place, keys, preferred_element_type=jnp.float32).astype(jnp.bfloat16)
    out[:, 0:16, :] = moved.reshape(16, 16, 128)
    out[:, 16:32, :] = named.reshape(16, 16, 128)


def pack_slots(live, rows, owner, deltas):
    vmem = pl.BlockSpec(memory_space=pltpu.VMEM)
    return pl.pallas_call(
        slots_kernel,
        out_shape=jax.ShapeDtypeStruct((16, 32, 128), jnp.bfloat16),
        in_specs=[pl.BlockSpec(memory_space=pltpu.SMEM), vmem, vmem, vmem, vmem],
        out_specs=vmem,
    )(live, rows.reshape(-1, 1), owner, owner.reshape(1, -1), deltas)


def grad_kernel(half, tokens, out):
    first = pl.multiple_of(half[0] * 128, 128)
    second = pl.multiple_of(256 + half[0] * 128, 128)
    left = jnp.concatenate(
        [
            tokens[:, 2, :, pl.ds(first, 128)].reshape(1024, 128),
            tokens[:, 2, :, pl.ds(second, 128)].reshape(1024, 128),
        ],
        axis=1,
    )
    for k in range(2):
        result = lax.dot_general(
            left,
            tokens[:, k, :, :].reshape(1024, 512),
            (((0,), (0,)), ((), ())),
            preferred_element_type=jnp.float32,
        )
        out[k] = result.reshape(2, 128, 512)


def partial_grads(half, tokens):
    return pl.pallas_call(
        grad_kernel,
        out_shape=jax.ShapeDtypeStruct((2, 2, 128, 512), jnp.float32),
        in_specs=[pl.BlockSpec(memory_space=pltpu.SMEM), pl.BlockSpec(memory_space=pltpu.VMEM)],
        out_specs=pl.BlockSpec(memory_space=pltpu.VMEM),
        compiler_params=pltpu.CompilerParams(vmem_limit_bytes=32 * MIB),
        cost_estimate=pl.CostEstimate(flops=1 << 29, bytes_accessed=4 * MIB, transcendentals=0),
    )(half, tokens)


def parts_of(value):
    high = value.astype(jnp.bfloat16)
    return high, (value - high.astype(jnp.float32)).astype(jnp.bfloat16)


def product(a, b, contract):
    return lax.dot_general(a, b, (contract, ((), ())), preferred_element_type=jnp.float32)


def full_product(a, b, contract):
    (ah, al), (bh, bl) = a, b
    return product(ah, bh, contract) + (product(ah, bl, contract) + product(al, bh, contract))


def rows_product(rows, b):
    bh, bl = b
    count = rows.shape[0]
    high, low = parts_of(rows)
    both = jnp.concatenate([high.astype(jnp.float32), low.astype(jnp.float32)], axis=0)
    first = product(both.astype(jnp.bfloat16), bh, ((1,), (0,)))
    return first[:count] + (first[count:] + product(high, bl, ((1,), (0,))))


def direction_kernel(place, own, other, out, grad, power, square):
    half, first_row = place[0], pl.multiple_of(place[1], 8)
    for k in range(2):
        grad[pl.ds(pl.multiple_of(k * 256 + half * 128, 128), 128), :] = own[k]
        grad[pl.ds(pl.multiple_of(k * 256 + (1 - half) * 128, 128), 128), :] = other[k]
    g = grad[...]
    width = g.shape[0]
    frobenius = jnp.sum(g * g) + 1e-06
    g_parts = parts_of(g)
    normal = full_product(g_parts, g_parts, ((1,), (1,))) / frobenius
    n_parts = parts_of(normal)
    squared = full_product(n_parts, n_parts, ((1,), (0,)))
    total = jnp.sum(jnp.sum(squared * squared, axis=0, keepdims=True), axis=1, keepdims=True)
    bound = jnp.sqrt(jnp.sqrt(total))
    scale = frobenius * bound
    m = normal / bound
    m2 = squared / (bound * bound)
    power[...] = m
    square[...] = m2
    diagonal = lax.broadcasted_iota(jnp.int32, (width, width), 0) == lax.broadcasted_iota(
        jnp.int32, (width, width), 1
    )
    f2 = (jnp.where(diagonal, 25.0, 0.0) - 10.0 * m + m2) / 16.0
    m_parts, f_parts = parts_of(m), parts_of(f2)
    m_rows = power[pl.ds(first_row, 8), :]
    m2_rows = square[pl.ds(first_row, 8), :]
    basis = lax.broadcasted_iota(jnp.int32, (8, width), 1) == first_row + lax.broadcasted_iota(
        jnp.int32, (8, width), 0
    )
    f_rows = (jnp.where(basis, 5.0, 0.0) - m_rows) / 4.0
    fm_rows = (5.0 * m_rows - m2_rows) / 4.0
    root = (5.0 * f_rows - rows_product(rows_product(fm_rows, f_parts), f_parts)) / 4.0
    m_root = rows_product(root, m_parts)
    m2_root = rows_product(m_root, m_parts)
    f_rows = (5.0 * root - m_root) / 4.0
    fm_rows = (5.0 * m_root - m2_root) / 4.0
    root = (5.0 * f_rows - rows_product(rows_product(fm_rows, f_parts), f_parts)) / 4.0
    quarter = 1.0 / jnp.sqrt(jnp.sqrt(scale))
    result = rows_product(root * quarter, g_parts) * quarter * float(width)
    tall = jnp.concatenate([result[:, t * 128 : (t + 1) * 128] for t in range(4)], axis=0)
    out[...] = tall.astype(jnp.bfloat16)


def direction_rows(place, own, other):
    vmem = pl.BlockSpec(memory_space=pltpu.VMEM)
    square = pltpu.VMEM((512, 512), jnp.float32)
    return pl.pallas_call(
        direction_kernel,
        out_shape=jax.ShapeDtypeStruct((32, 128), jnp.bfloat16),
        in_specs=[pl.BlockSpec(memory_space=pltpu.SMEM), vmem, vmem],
        out_specs=vmem,
        scratch_shapes=[square, square, square],
        compiler_params=pltpu.CompilerParams(vmem_limit_bytes=40 * MIB),
    )(place, own, other)


def message_kernel(rows, slots, out):
    for target in range(16):
        out[target, 0:32, :] = rows[...]
    out[:, 32:64, :] = slots[...]


def final_message(rows, slots):
    vmem = pl.BlockSpec(memory_space=pltpu.VMEM)
    return pl.pallas_call(
        message_kernel,
        out_shape=jax.ShapeDtypeStruct((16, 64, 128), jnp.bfloat16),
        in_specs=[vmem, vmem],
        out_specs=vmem,
    )(rows, slots)


def update_kernel(got, table, accum, new_table, new_accum, directions):
    rows = got[:, 0:32, :].astype(jnp.float32).reshape(16, 4, 8, 128)
    wide = jnp.concatenate([rows[:, t] for t in range(4)], axis=2)
    directions[...] = wide.astype(jnp.bfloat16)
    deltas = got[:, 32:48, :].reshape(256, 128)
    keys = got[:, 48:64, :].astype(jnp.float32).reshape(256, 128)
    row = keys[:, 0:1] * 16.0 + keys[:, 64:65]
    count = table.shape[0]
    named = row == lax.broadcasted_iota(jnp.int32, (256, count), 1).astype(jnp.float32)
    named = named.astype(jnp.float32).astype(jnp.bfloat16)
    summed = lax.dot_general(
        named, deltas, (((0,), (0,)), ((), ())), preferred_element_type=jnp.float32
    )
    before = jnp.transpose(jnp.broadcast_to(accum[...], (128, count)))
    after = before + jnp.sum(summed * summed, axis=1, keepdims=True) / 128.0
    new_table[...] = table[...] - summed / jnp.sqrt(after)
    new_accum[...] = jnp.transpose(after)[0:1, :]


def update_rows(got, table, accum):
    vmem = pl.BlockSpec(memory_space=pltpu.VMEM)
    return pl.pallas_call(
        update_kernel,
        out_shape=(
            jax.ShapeDtypeStruct(table.shape, jnp.float32),
            jax.ShapeDtypeStruct((1, accum.shape[0]), jnp.float32),
            jax.ShapeDtypeStruct((16, 8, 512), jnp.bfloat16),
        ),
        in_specs=[vmem, vmem, vmem],
        out_specs=(vmem, vmem, vmem),
    )(got, table, accum.reshape(1, -1))


def shards(
    features,
    output_grads,
    block_order,
    emb_table,
    row_accum,
    hot_rows,
    hot_owner,
    live_counts,
    hot_deltas,
):
    group, replica = lax.axis_index("grp"), lax.axis_index("rep")
    core, z = group % 2, group // 2
    x, y = replica // SIDE, replica % SIDE
    exchange = partial(lax.all_to_all, split_axis=0, concat_axis=0, tiled=True)

    slots = pack_slots(live_counts, hot_rows, hot_owner, hot_deltas)

    message = pack_tokens(block_order, output_grads, features)
    tokens = exchange(message, AXES, axis_index_groups=cube_groups())

    away = partial_grads((1 - core).reshape(1), tokens)
    arrived = lax.ppermute(away, AXES, core_pairs())
    kept = partial_grads(core.reshape(1), tokens)
    shared = (kept + arrived).reshape(64, 8, 512)
    terms = exchange(shared, AXES, axis_index_groups=stride_groups(False))
    reduced = jnp.sum(terms, axis=0)

    spread = jnp.broadcast_to(reduced[None], (32, 8, 512))
    own = exchange(spread, AXES, axis_index_groups=stride_groups(True)).reshape(2, 128, 512)
    other = lax.ppermute(own, AXES, core_pairs())
    turn = piece(x, y, z)
    first_row = (turn // 16) * 256 + core * 128 + (turn % 16) * 8
    rows = direction_rows(jnp.stack([core, first_row]).astype(jnp.int32), own, other)

    home = lax.ppermute(rows, AXES, home_pairs())
    got = exchange(final_message(home, slots), "grp")
    new_table, new_accum, directions = update_rows(got, emb_table, row_accum)
    return (new_table, new_accum.reshape(-1), directions)


def solution(mesh):
    return jax.shard_map(
        shards,
        mesh=mesh,
        in_specs=(
            P(AXES, None),
            P(AXES, None),
            P(),
            P(AXES, None),
            P(AXES),
            P(AXES),
            P(AXES, None),
            P(AXES),
            P(AXES, None),
        ),
        out_specs=(P(AXES, None), P(AXES), P(None, "rep", None)),
        check_vma=False,
    )
```

```python
from functools import partial

import jax
import jax.numpy as jnp
from jax import lax
from jax.experimental import pallas as pl
from jax.experimental.pallas import tpu as pltpu
from jax.sharding import PartitionSpec as P

SIDE = 8
AXES = ("grp", "rep")
MIB = 1 << 20


def device(x, y, z, core):
    return ((z % SIDE) * 2 + core) * (SIDE * SIDE) + (x % SIDE) * SIDE + y % SIDE


def chips():
    for x in range(SIDE):
        for y in range(SIDE):
            for z in range(SIDE):
                yield x, y, z


def parity(x, y, z):
    return (y % 2) * 4 + (z % 2) * 2 + x % 2


def cube_groups():
    groups = []
    for core in range(2):
        for x, y, z in chips():
            if x % 2 != core or y % 2 != core or z % 2 != core:
                continue
            members = [None] * 8
            for dx in range(2):
                for dy in range(2):
                    for dz in range(2):
                        spot = ((x + dx) % SIDE, (y + dy) % SIDE, (z + dz) % SIDE)
                        members[parity(*spot)] = device(*spot, core)
            groups.append(members)
    return groups


def piece(x, y, z):
    return (((x // 2) * 4 + y // 2) * 2) + (z // 2) % 2


def stride_groups(split):
    groups = {}
    for core in range(2):
        for x, y, z in chips():
            half = z // 4
            key = (core, parity(x, y, z)) + ((half,) if split else ())
            order = piece(x, y, z) + (0 if split else 32 * half)
            groups.setdefault(key, []).append((order, device(x, y, z, core)))
    return [[d for _, d in sorted(members)] for members in groups.values()]


def core_pairs():
    return [(device(x, y, z, c), device(x, y, z, 1 - c)) for x, y, z in chips() for c in range(2)]


def home_pairs():
    pairs = []
    for x, y, z in chips():
        for core in range(2):
            to_x = (x & 4) | (core << 1) | ((x >> 1) & 1)
            to_y = (y & 6) | ((z >> 1) & 1)
            to_z = (z & 5) | ((y & 1) << 1)
            pairs.append((device(x, y, z, core), device(to_x, to_y, to_z, x & 1)))
    return pairs


def tokens_kernel(order, grads, features, out):
    for spot in range(8):
        for k in range(2):
            first = pl.multiple_of(order[spot + 8 * k] * 512, 512)
            out[spot, k] = grads[:, pl.ds(first, 512)]
        out[spot, 2] = features[...]


def pack_tokens(order, grads, features):
    vmem = pl.BlockSpec(memory_space=pltpu.VMEM)
    return pl.pallas_call(
        tokens_kernel,
        out_shape=jax.ShapeDtypeStruct((8, 3, 128, 512), jnp.bfloat16),
        in_specs=[pl.BlockSpec(memory_space=pltpu.SMEM), vmem, vmem],
        out_specs=vmem,
        compiler_params=pltpu.CompilerParams(vmem_limit_bytes=32 * MIB),
    )(order, grads, features)


def slots_kernel(live, rows, owner_col, owner_row, deltas, out):
    count = deltas.shape[0]
    before = lax.broadcasted_iota(jnp.int32, (count, count), 0)
    after = lax.broadcasted_iota(jnp.int32, (count, count), 1)
    same = (owner_col[...] == owner_row[...]) & (before < after)
    rank = jnp.sum(same.astype(jnp.float32), axis=0, keepdims=True)
    position = owner_row[...].astype(jnp.float32) * 16.0 + rank
    place = lax.broadcasted_iota(jnp.int32, (256, count), 0).astype(jnp.float32) == position
    place = place.astype(jnp.float32).astype(jnp.bfloat16)
    masked = jnp.where(before < live[0], deltas[...].astype(jnp.float32), 0.0).astype(jnp.bfloat16)
    high, low = rows[...] // 16, rows[...] % 16
    keys = jnp.where(after < 64, high, low).astype(jnp.float32).astype(jnp.bfloat16)
    moved = jnp.dot(place, masked, preferred_element_type=jnp.float32).astype(jnp.bfloat16)
    named = jnp.dot(place, keys, preferred_element_type=jnp.float32).astype(jnp.bfloat16)
    out[:, 0:16, :] = moved.reshape(16, 16, 128)
    out[:, 16:32, :] = named.reshape(16, 16, 128)


def pack_slots(live, rows, owner, deltas):
    vmem = pl.BlockSpec(memory_space=pltpu.VMEM)
    return pl.pallas_call(
        slots_kernel,
        out_shape=jax.ShapeDtypeStruct((16, 32, 128), jnp.bfloat16),
        in_specs=[pl.BlockSpec(memory_space=pltpu.SMEM), vmem, vmem, vmem, vmem],
        out_specs=vmem,
    )(live, rows.reshape(-1, 1), owner, owner.reshape(1, -1), deltas)


def grad_kernel(half, tokens, out):
    first = pl.multiple_of(half[0] * 128, 128)
    second = pl.multiple_of(256 + half[0] * 128, 128)
    left = jnp.concatenate(
        [
            tokens[:, 2, :, pl.ds(first, 128)].reshape(1024, 128),
            tokens[:, 2, :, pl.ds(second, 128)].reshape(1024, 128),
        ],
        axis=1,
    )
    for k in range(2):
        result = lax.dot_general(
            left,
            tokens[:, k, :, :].reshape(1024, 512),
            (((0,), (0,)), ((), ())),
            preferred_element_type=jnp.float32,
        )
        out[k] = result.reshape(2, 128, 512)


def partial_grads(half, tokens):
    return pl.pallas_call(
        grad_kernel,
        out_shape=jax.ShapeDtypeStruct((2, 2, 128, 512), jnp.float32),
        in_specs=[pl.BlockSpec(memory_space=pltpu.SMEM), pl.BlockSpec(memory_space=pltpu.VMEM)],
        out_specs=pl.BlockSpec(memory_space=pltpu.VMEM),
        compiler_params=pltpu.CompilerParams(vmem_limit_bytes=32 * MIB),
        cost_estimate=pl.CostEstimate(flops=1 << 29, bytes_accessed=4 * MIB, transcendentals=0),
    )(half, tokens)


def parts_of(value):
    high = value.astype(jnp.bfloat16)
    return high, (value - high.astype(jnp.float32)).astype(jnp.bfloat16)


def product(a, b, contract):
    return lax.dot_general(a, b, (contract, ((), ())), preferred_element_type=jnp.float32)


def full_product(a, b, contract):
    (ah, al), (bh, bl) = a, b
    return product(ah, bh, contract) + (product(ah, bl, contract) + product(al, bh, contract))


def rows_product(rows, b):
    bh, bl = b
    count = rows.shape[0]
    high, low = parts_of(rows)
    both = jnp.concatenate([high.astype(jnp.float32), low.astype(jnp.float32)], axis=0)
    first = product(both.astype(jnp.bfloat16), bh, ((1,), (0,)))
    return first[:count] + (first[count:] + product(high, bl, ((1,), (0,))))


def direction_kernel(place, own, other, out, grad, power, square):
    half, first_row = place[0], pl.multiple_of(place[1], 8)
    for k in range(2):
        grad[pl.ds(pl.multiple_of(k * 256 + half * 128, 128), 128), :] = own[k]
        grad[pl.ds(pl.multiple_of(k * 256 + (1 - half) * 128, 128), 128), :] = other[k]
    g = grad[...]
    width = g.shape[0]
    frobenius = jnp.sum(g * g) + 1e-06
    g_parts = parts_of(g)
    normal = full_product(g_parts, g_parts, ((1,), (1,))) / frobenius
    n_parts = parts_of(normal)
    squared = full_product(n_parts, n_parts, ((1,), (0,)))
    total = jnp.sum(jnp.sum(squared * squared, axis=0, keepdims=True), axis=1, keepdims=True)
    bound = jnp.sqrt(jnp.sqrt(total))
    scale = frobenius * bound
    m = normal / bound
    m2 = squared / (bound * bound)
    power[...] = m
    square[...] = m2
    diagonal = lax.broadcasted_iota(jnp.int32, (width, width), 0) == lax.broadcasted_iota(
        jnp.int32, (width, width), 1
    )
    f2 = (jnp.where(diagonal, 25.0, 0.0) - 10.0 * m + m2) / 16.0
    m_parts, f_parts = parts_of(m), parts_of(f2)
    m_rows = power[pl.ds(first_row, 8), :]
    m2_rows = square[pl.ds(first_row, 8), :]
    basis = lax.broadcasted_iota(jnp.int32, (8, width), 1) == first_row + lax.broadcasted_iota(
        jnp.int32, (8, width), 0
    )
    f_rows = (jnp.where(basis, 5.0, 0.0) - m_rows) / 4.0
    fm_rows = (5.0 * m_rows - m2_rows) / 4.0
    root = (5.0 * f_rows - rows_product(rows_product(fm_rows, f_parts), f_parts)) / 4.0
    m_root = rows_product(root, m_parts)
    m2_root = rows_product(m_root, m_parts)
    f_rows = (5.0 * root - m_root) / 4.0
    fm_rows = (5.0 * m_root - m2_root) / 4.0
    root = (5.0 * f_rows - rows_product(rows_product(fm_rows, f_parts), f_parts)) / 4.0
    quarter = 1.0 / jnp.sqrt(jnp.sqrt(scale))
    result = rows_product(root * quarter, g_parts) * quarter * float(width)
    tall = jnp.concatenate([result[:, t * 128 : (t + 1) * 128] for t in range(4)], axis=0)
    out[...] = tall.astype(jnp.bfloat16)


def direction_rows(place, own, other):
    vmem = pl.BlockSpec(memory_space=pltpu.VMEM)
    square = pltpu.VMEM((512, 512), jnp.float32)
    return pl.pallas_call(
        direction_kernel,
        out_shape=jax.ShapeDtypeStruct((32, 128), jnp.bfloat16),
        in_specs=[pl.BlockSpec(memory_space=pltpu.SMEM), vmem, vmem],
        out_specs=vmem,
        scratch_shapes=[square, square, square],
        compiler_params=pltpu.CompilerParams(vmem_limit_bytes=40 * MIB),
    )(place, own, other)


def message_kernel(rows, slots, out):
    for target in range(16):
        out[target, 0:32, :] = rows[...]
    out[:, 32:64, :] = slots[...]


def final_message(rows, slots):
    vmem = pl.BlockSpec(memory_space=pltpu.VMEM)
    return pl.pallas_call(
        message_kernel,
        out_shape=jax.ShapeDtypeStruct((16, 64, 128), jnp.bfloat16),
        in_specs=[vmem, vmem],
        out_specs=vmem,
    )(rows, slots)


def update_kernel(got, table, accum, new_table, new_accum, directions):
    rows = got[:, 0:32, :].astype(jnp.float32).reshape(16, 4, 8, 128)
    wide = jnp.concatenate([rows[:, t] for t in range(4)], axis=2)
    directions[...] = wide.astype(jnp.bfloat16)
    deltas = got[:, 32:48, :].reshape(256, 128)
    keys = got[:, 48:64, :].astype(jnp.float32).reshape(256, 128)
    row = keys[:, 0:1] * 16.0 + keys[:, 64:65]
    count = table.shape[0]
    named = row == lax.broadcasted_iota(jnp.int32, (256, count), 1).astype(jnp.float32)
    named = named.astype(jnp.float32).astype(jnp.bfloat16)
    summed = lax.dot_general(
        named, deltas, (((0,), (0,)), ((), ())), preferred_element_type=jnp.float32
    )
    before = jnp.transpose(jnp.broadcast_to(accum[...], (128, count)))
    after = before + jnp.sum(summed * summed, axis=1, keepdims=True) / 128.0
    new_table[...] = table[...] - summed / jnp.sqrt(after)
    new_accum[...] = jnp.transpose(after)[0:1, :]


def update_rows(got, table, accum):
    vmem = pl.BlockSpec(memory_space=pltpu.VMEM)
    return pl.pallas_call(
        update_kernel,
        out_shape=(
            jax.ShapeDtypeStruct(table.shape, jnp.float32),
            jax.ShapeDtypeStruct((1, accum.shape[0]), jnp.float32),
            jax.ShapeDtypeStruct((16, 8, 512), jnp.bfloat16),
        ),
        in_specs=[vmem, vmem, vmem],
        out_specs=(vmem, vmem, vmem),
    )(got, table, accum.reshape(1, -1))


def shards(
    features,
    output_grads,
    block_order,
    emb_table,
    row_accum,
    hot_rows,
    hot_owner,
    live_counts,
    hot_deltas,
):
    group, replica = lax.axis_index("grp"), lax.axis_index("rep")
    core, z = group % 2, group // 2
    x, y = replica // SIDE, replica % SIDE
    exchange = partial(lax.all_to_all, split_axis=0, concat_axis=0, tiled=True)

    slots = pack_slots(live_counts, hot_rows, hot_owner, hot_deltas)

    message = pack_tokens(block_order, output_grads, features)
    tokens = exchange(message, AXES, axis_index_groups=cube_groups())
    tokens, slots = lax.optimization_barrier((tokens, slots))

    away = partial_grads((1 - core).reshape(1), tokens)
    arrived = lax.ppermute(away, AXES, core_pairs())
    kept = partial_grads(core.reshape(1), tokens)
    shared = (kept + arrived).reshape(64, 8, 512)
    terms = exchange(shared, AXES, axis_index_groups=stride_groups(False))
    reduced = jnp.sum(terms, axis=0)

    spread = jnp.broadcast_to(reduced[None], (32, 8, 512))
    own = exchange(spread, AXES, axis_index_groups=stride_groups(True)).reshape(2, 128, 512)
    other = lax.ppermute(own, AXES, core_pairs())
    turn = piece(x, y, z)
    first_row = (turn // 16) * 256 + core * 128 + (turn % 16) * 8
    rows = direction_rows(jnp.stack([core, first_row]).astype(jnp.int32), own, other)

    home = lax.ppermute(rows, AXES, home_pairs())
    got = exchange(final_message(home, slots), "grp")
    new_table, new_accum, directions = update_rows(got, emb_table, row_accum)
    return (new_table, new_accum.reshape(-1), directions)


def solution(mesh):
    return jax.shard_map(
        shards,
        mesh=mesh,
        in_specs=(
            P(AXES, None),
            P(AXES, None),
            P(),
            P(AXES, None),
            P(AXES),
            P(AXES),
            P(AXES, None),
            P(AXES),
            P(AXES, None),
        ),
        out_specs=(P(AXES, None), P(AXES), P(None, "rep", None)),
        check_vma=False,
    )
```

```python
from functools import partial

import jax
import jax.numpy as jnp
from jax import lax
from jax.experimental import pallas as pl
from jax.experimental.pallas import tpu as pltpu
from jax.sharding import PartitionSpec as P

SIDE = 8
AXES = ("grp", "rep")
MIB = 1 << 20
CODE_RANGE = float((1 << 19) - 1)


def device(x, y, z, core):
    return ((z % SIDE) * 2 + core) * (SIDE * SIDE) + (x % SIDE) * SIDE + y % SIDE


def chips():
    for x in range(SIDE):
        for y in range(SIDE):
            for z in range(SIDE):
                yield x, y, z


def parity(x, y, z):
    return (y % 2) * 4 + (z % 2) * 2 + x % 2


def cube_groups():
    groups = []
    for core in range(2):
        for x, y, z in chips():
            if x % 2 != core or y % 2 != core or z % 2 != core:
                continue
            members = [None] * 8
            for dx in range(2):
                for dy in range(2):
                    for dz in range(2):
                        spot = ((x + dx) % SIDE, (y + dy) % SIDE, (z + dz) % SIDE)
                        members[parity(*spot)] = device(*spot, core)
            groups.append(members)
    return groups


def piece(x, y, z):
    return (((x // 2) * 4 + y // 2) * 2) + (z // 2) % 2


def stride_groups(split):
    groups = {}
    for core in range(2):
        for x, y, z in chips():
            half = z // 4
            key = (core, parity(x, y, z)) + ((half,) if split else ())
            order = piece(x, y, z) + (0 if split else 32 * half)
            groups.setdefault(key, []).append((order, device(x, y, z, core)))
    return [[d for _, d in sorted(members)] for members in groups.values()]


def core_pairs():
    return [(device(x, y, z, c), device(x, y, z, 1 - c)) for x, y, z in chips() for c in range(2)]


def home_pairs():
    pairs = []
    for x, y, z in chips():
        for core in range(2):
            to_x = (x & 4) | (core << 1) | ((x >> 1) & 1)
            to_y = (y & 6) | ((z >> 1) & 1)
            to_z = (z & 5) | ((y & 1) << 1)
            pairs.append((device(x, y, z, core), device(to_x, to_y, to_z, x & 1)))
    return pairs


def tokens_kernel(order, grads, features, out, held, arrive, leave):
    copies = []
    for spot in range(8):
        for k in range(2):
            first = pl.multiple_of(order[spot + 8 * k] * 512, 512)
            copies.append((grads.at[:, pl.ds(first, 512)], spot, k))
        copies.append((features, spot, 2))
    coming = []
    for n, (source, spot, k) in enumerate(copies):
        copy = pltpu.make_async_copy(source, held.at[spot, k], arrive.at[n])
        copy.start()
        coming.append(copy)
    going = []
    for n, (source, spot, k) in enumerate(copies):
        coming[n].wait()
        copy = pltpu.make_async_copy(held.at[spot, k], out.at[spot, k], leave.at[n])
        copy.start()
        going.append(copy)
    for copy in going:
        copy.wait()


def pack_tokens(order, grads, features):
    shape = (8, 3, 128, 512)
    hbm = pl.BlockSpec(memory_space=pltpu.HBM)
    return pl.pallas_call(
        tokens_kernel,
        out_shape=jax.ShapeDtypeStruct(shape, jnp.bfloat16),
        in_specs=[pl.BlockSpec(memory_space=pltpu.SMEM), hbm, hbm],
        out_specs=hbm,
        scratch_shapes=[
            pltpu.VMEM(shape, jnp.bfloat16),
            pltpu.SemaphoreType.DMA((24,)),
            pltpu.SemaphoreType.DMA((24,)),
        ],
        compiler_params=pltpu.CompilerParams(vmem_limit_bytes=16 * MIB),
    )(order, grads, features)


def slots_kernel(live, rows, owner_col, owner_row, deltas, out):
    count = deltas.shape[0]
    before = lax.broadcasted_iota(jnp.int32, (count, count), 0)
    after = lax.broadcasted_iota(jnp.int32, (count, count), 1)
    same = (owner_col[...] == owner_row[...]) & (before < after)
    rank = jnp.sum(same.astype(jnp.float32), axis=0, keepdims=True)
    position = owner_row[...].astype(jnp.float32) * 16.0 + rank
    place = lax.broadcasted_iota(jnp.int32, (256, count), 0).astype(jnp.float32) == position
    place = place.astype(jnp.float32).astype(jnp.bfloat16)
    masked = jnp.where(before < live[0], deltas[...].astype(jnp.float32), 0.0).astype(jnp.bfloat16)
    high, low = rows[...] // 16, rows[...] % 16
    keys = jnp.where(after < 64, high, low).astype(jnp.float32).astype(jnp.bfloat16)
    moved = jnp.dot(place, masked, preferred_element_type=jnp.float32).astype(jnp.bfloat16)
    named = jnp.dot(place, keys, preferred_element_type=jnp.float32).astype(jnp.bfloat16)
    out[:, 0:16, :] = moved.reshape(16, 16, 128)
    out[:, 16:32, :] = named.reshape(16, 16, 128)


def pack_slots(live, rows, owner, deltas):
    vmem = pl.BlockSpec(memory_space=pltpu.VMEM)
    return pl.pallas_call(
        slots_kernel,
        out_shape=jax.ShapeDtypeStruct((16, 32, 128), jnp.bfloat16),
        in_specs=[pl.BlockSpec(memory_space=pltpu.SMEM), vmem, vmem, vmem, vmem],
        out_specs=vmem,
    )(live, rows.reshape(-1, 1), owner, owner.reshape(1, -1), deltas)


def grad_kernel(half, tokens, out):
    first = pl.multiple_of(half[0] * 128, 128)
    second = pl.multiple_of(256 + half[0] * 128, 128)
    left = jnp.concatenate(
        [
            tokens[:, 2, :, pl.ds(first, 128)].reshape(1024, 128),
            tokens[:, 2, :, pl.ds(second, 128)].reshape(1024, 128),
        ],
        axis=1,
    )
    for k in range(2):
        result = lax.dot_general(
            left,
            tokens[:, k, :, :].reshape(1024, 512),
            (((0,), (0,)), ((), ())),
            preferred_element_type=jnp.float32,
        )
        out[k] = result.reshape(2, 128, 512)


def partial_grads(half, tokens):
    return pl.pallas_call(
        grad_kernel,
        out_shape=jax.ShapeDtypeStruct((2, 2, 128, 512), jnp.float32),
        in_specs=[pl.BlockSpec(memory_space=pltpu.SMEM), pl.BlockSpec(memory_space=pltpu.VMEM)],
        out_specs=pl.BlockSpec(memory_space=pltpu.VMEM),
        compiler_params=pltpu.CompilerParams(vmem_limit_bytes=32 * MIB),
        cost_estimate=pl.CostEstimate(flops=1 << 29, bytes_accessed=4 * MIB, transcendentals=0),
    )(half, tokens)


def encode(tiles):
    largest = jnp.abs(tiles[0])
    for tile in tiles[1:]:
        largest = jnp.maximum(largest, jnp.abs(tile))
    largest = jnp.max(jnp.max(largest, axis=1, keepdims=True), axis=2, keepdims=True)
    grade = jnp.ceil(8.0 * jnp.log2(jnp.maximum(largest, 1e-30))) + 1.0
    factor = CODE_RANGE * jnp.exp2(grade * -0.125)
    words, low = [], None
    for t, tile in enumerate(tiles):
        whole = jnp.round(jnp.clip(tile * factor, -CODE_RANGE, CODE_RANGE)).astype(jnp.int32)
        words.append(whole >> 4)
        nibble = (whole & 15) << (4 * t)
        low = nibble if low is None else low | nibble
    spot = lax.broadcasted_iota(jnp.int32, low.shape, 1) + lax.broadcasted_iota(
        jnp.int32, low.shape, 2
    )
    words.append(jnp.where(spot == 0, grade.astype(jnp.int32), low))
    return jnp.concatenate(words, axis=1).astype(jnp.int16)


def decode(words):
    words = words.astype(jnp.int32)
    low = words[:, 32:40, :]
    grade = low[:, 0:1, 0:1].astype(jnp.float32)
    factor = jnp.exp2(grade * 0.125) * (1.0 / CODE_RANGE)
    tiles = []
    for t in range(4):
        whole = words[:, 8 * t : 8 * t + 8, :] * 16 + ((low >> (4 * t)) & 15)
        tiles.append(whole.astype(jnp.float32) * factor)
    return tiles


def share_kernel(kept, arrived, out):
    tiles = []
    for t in range(4):
        cut = slice(t * 128, (t + 1) * 128)
        tiles.append((kept[:, :, :, cut] + arrived[:, :, :, cut]).reshape(64, 8, 128))
    out[...] = encode(tiles)


def share(kept, arrived):
    vmem = pl.BlockSpec(memory_space=pltpu.VMEM)
    return pl.pallas_call(
        share_kernel,
        out_shape=jax.ShapeDtypeStruct((64, 40, 128), jnp.int16),
        in_specs=[vmem, vmem],
        out_specs=vmem,
        compiler_params=pltpu.CompilerParams(vmem_limit_bytes=32 * MIB),
    )(kept, arrived)


def total_kernel(terms, out):
    words = encode([jnp.sum(tile, axis=0, keepdims=True) for tile in decode(terms[...])])
    out[...] = jnp.broadcast_to(words.astype(jnp.int32), (32, 40, 128)).astype(jnp.int16)


def total(terms):
    vmem = pl.BlockSpec(memory_space=pltpu.VMEM)
    return pl.pallas_call(
        total_kernel,
        out_shape=jax.ShapeDtypeStruct((32, 40, 128), jnp.int16),
        in_specs=[vmem],
        out_specs=vmem,
        compiler_params=pltpu.CompilerParams(vmem_limit_bytes=32 * MIB),
    )(terms)


def parts_of(value):
    high = value.astype(jnp.bfloat16)
    return high, (value - high.astype(jnp.float32)).astype(jnp.bfloat16)


def product(a, b, contract):
    return lax.dot_general(a, b, (contract, ((), ())), preferred_element_type=jnp.float32)


def full_product(a, b, contract):
    (ah, al), (bh, bl) = a, b
    return product(ah, bh, contract) + (product(ah, bl, contract) + product(al, bh, contract))


def rows_product(rows, b):
    bh, bl = b
    count = rows.shape[0]
    high, low = parts_of(rows)
    both = jnp.concatenate([high.astype(jnp.float32), low.astype(jnp.float32)], axis=0)
    first = product(both.astype(jnp.bfloat16), bh, ((1,), (0,)))
    return first[:count] + (first[count:] + product(high, bl, ((1,), (0,))))


def direction_kernel(place, own, other, out, grad, power, square):
    half, first_row = place[0], pl.multiple_of(place[1], 8)
    for side, words in ((half, own), (1 - half, other)):
        for t, tile in enumerate(decode(words[...])):
            tile = tile.reshape(2, 128, 128)
            for k in range(2):
                rows = pl.ds(pl.multiple_of(k * 256 + side * 128, 128), 128)
                grad[rows, t * 128 : (t + 1) * 128] = tile[k]
    g = grad[...]
    width = g.shape[0]
    frobenius = jnp.sum(g * g) + 1e-06
    g_parts = parts_of(g)
    normal = full_product(g_parts, g_parts, ((1,), (1,))) / frobenius
    n_parts = parts_of(normal)
    squared = full_product(n_parts, n_parts, ((1,), (0,)))
    total = jnp.sum(jnp.sum(squared * squared, axis=0, keepdims=True), axis=1, keepdims=True)
    bound = jnp.sqrt(jnp.sqrt(total))
    scale = frobenius * bound
    m = normal / bound
    m2 = squared / (bound * bound)
    power[...] = m
    square[...] = m2
    diagonal = lax.broadcasted_iota(jnp.int32, (width, width), 0) == lax.broadcasted_iota(
        jnp.int32, (width, width), 1
    )
    f2 = (jnp.where(diagonal, 25.0, 0.0) - 10.0 * m + m2) / 16.0
    m_parts, f_parts = parts_of(m), parts_of(f2)
    m_rows = power[pl.ds(first_row, 8), :]
    m2_rows = square[pl.ds(first_row, 8), :]
    basis = lax.broadcasted_iota(jnp.int32, (8, width), 1) == first_row + lax.broadcasted_iota(
        jnp.int32, (8, width), 0
    )
    f_rows = (jnp.where(basis, 5.0, 0.0) - m_rows) / 4.0
    fm_rows = (5.0 * m_rows - m2_rows) / 4.0
    root = (5.0 * f_rows - rows_product(rows_product(fm_rows, f_parts), f_parts)) / 4.0
    m_root = rows_product(root, m_parts)
    m2_root = rows_product(m_root, m_parts)
    f_rows = (5.0 * root - m_root) / 4.0
    fm_rows = (5.0 * m_root - m2_root) / 4.0
    root = (5.0 * f_rows - rows_product(rows_product(fm_rows, f_parts), f_parts)) / 4.0
    quarter = 1.0 / jnp.sqrt(jnp.sqrt(scale))
    result = rows_product(root * quarter, g_parts) * quarter * float(width)
    tall = jnp.concatenate([result[:, t * 128 : (t + 1) * 128] for t in range(4)], axis=0)
    out[...] = tall.astype(jnp.bfloat16)


def direction_rows(place, own, other):
    vmem = pl.BlockSpec(memory_space=pltpu.VMEM)
    square = pltpu.VMEM((512, 512), jnp.float32)
    return pl.pallas_call(
        direction_kernel,
        out_shape=jax.ShapeDtypeStruct((32, 128), jnp.bfloat16),
        in_specs=[pl.BlockSpec(memory_space=pltpu.SMEM), vmem, vmem],
        out_specs=vmem,
        scratch_shapes=[square, square, square],
        compiler_params=pltpu.CompilerParams(vmem_limit_bytes=40 * MIB),
    )(place, own, other)


def message_kernel(rows, slots, out):
    for target in range(16):
        out[target, 0:32, :] = rows[...]
    out[:, 32:64, :] = slots[...]


def final_message(rows, slots):
    vmem = pl.BlockSpec(memory_space=pltpu.VMEM)
    return pl.pallas_call(
        message_kernel,
        out_shape=jax.ShapeDtypeStruct((16, 64, 128), jnp.bfloat16),
        in_specs=[vmem, vmem],
        out_specs=vmem,
    )(rows, slots)


def update_kernel(got, table, accum, new_table, new_accum, directions):
    rows = got[:, 0:32, :].astype(jnp.float32).reshape(16, 4, 8, 128)
    wide = jnp.concatenate([rows[:, t] for t in range(4)], axis=2)
    directions[...] = wide.astype(jnp.bfloat16)
    deltas = got[:, 32:48, :].reshape(256, 128)
    keys = got[:, 48:64, :].astype(jnp.float32).reshape(256, 128)
    row = keys[:, 0:1] * 16.0 + keys[:, 64:65]
    count = table.shape[0]
    named = row == lax.broadcasted_iota(jnp.int32, (256, count), 1).astype(jnp.float32)
    named = named.astype(jnp.float32).astype(jnp.bfloat16)
    summed = lax.dot_general(
        named, deltas, (((0,), (0,)), ((), ())), preferred_element_type=jnp.float32
    )
    before = jnp.transpose(jnp.broadcast_to(accum[...], (128, count)))
    after = before + jnp.sum(summed * summed, axis=1, keepdims=True) / 128.0
    new_table[...] = table[...] - summed / jnp.sqrt(after)
    new_accum[...] = jnp.transpose(after)[0:1, :]


def update_rows(got, table, accum):
    vmem = pl.BlockSpec(memory_space=pltpu.VMEM)
    return pl.pallas_call(
        update_kernel,
        out_shape=(
            jax.ShapeDtypeStruct(table.shape, jnp.float32),
            jax.ShapeDtypeStruct((1, accum.shape[0]), jnp.float32),
            jax.ShapeDtypeStruct((16, 8, 512), jnp.bfloat16),
        ),
        in_specs=[vmem, vmem, vmem],
        out_specs=(vmem, vmem, vmem),
    )(got, table, accum.reshape(1, -1))


def shards(
    features,
    output_grads,
    block_order,
    emb_table,
    row_accum,
    hot_rows,
    hot_owner,
    live_counts,
    hot_deltas,
):
    group, replica = lax.axis_index("grp"), lax.axis_index("rep")
    core, z = group % 2, group // 2
    x, y = replica // SIDE, replica % SIDE
    exchange = partial(lax.all_to_all, split_axis=0, concat_axis=0, tiled=True)

    slots = pack_slots(live_counts, hot_rows, hot_owner, hot_deltas)

    message = pack_tokens(block_order, output_grads, features)
    tokens = exchange(message, AXES, axis_index_groups=cube_groups())
    tokens, slots = lax.optimization_barrier((tokens, slots))

    away = partial_grads((1 - core).reshape(1), tokens)
    arrived = lax.ppermute(away, AXES, core_pairs())
    kept = partial_grads(core.reshape(1), tokens)
    terms = exchange(share(kept, arrived), AXES, axis_index_groups=stride_groups(False))
    own = exchange(total(terms), AXES, axis_index_groups=stride_groups(True))
    other = lax.ppermute(own, AXES, core_pairs())
    turn = piece(x, y, z)
    first_row = (turn // 16) * 256 + core * 128 + (turn % 16) * 8
    rows = direction_rows(jnp.stack([core, first_row]).astype(jnp.int32), own, other)

    home = lax.ppermute(rows, AXES, home_pairs())
    got = exchange(final_message(home, slots), "grp")
    new_table, new_accum, directions = update_rows(got, emb_table, row_accum)
    return (new_table, new_accum.reshape(-1), directions)


def solution(mesh):
    return jax.shard_map(
        shards,
        mesh=mesh,
        in_specs=(
            P(AXES, None),
            P(AXES, None),
            P(),
            P(AXES, None),
            P(AXES),
            P(AXES),
            P(AXES, None),
            P(AXES),
            P(AXES, None),
        ),
        out_specs=(P(AXES, None), P(AXES), P(None, "rep", None)),
        check_vma=False,
    )
```

```python
from functools import partial

import jax
import jax.numpy as jnp
from jax import lax
from jax.experimental import pallas as pl
from jax.experimental.pallas import tpu as pltpu
from jax.sharding import PartitionSpec as P

SIDE = 8
AXES = ("grp", "rep")
MIB = 1 << 20
CODE_RANGE = float((1 << 19) - 1)


def device(x, y, z, core):
    return ((z % SIDE) * 2 + core) * (SIDE * SIDE) + (x % SIDE) * SIDE + y % SIDE


def chips():
    for x in range(SIDE):
        for y in range(SIDE):
            for z in range(SIDE):
                yield x, y, z


def parity(x, y, z):
    return (y % 2) * 4 + (z % 2) * 2 + x % 2


def cube_groups():
    groups = []
    for core in range(2):
        for x, y, z in chips():
            if x % 2 != core or y % 2 != core or z % 2 != core:
                continue
            members = [None] * 8
            for dx in range(2):
                for dy in range(2):
                    for dz in range(2):
                        spot = ((x + dx) % SIDE, (y + dy) % SIDE, (z + dz) % SIDE)
                        members[parity(*spot)] = device(*spot, core)
            groups.append(members)
    return groups


def piece(x, y, z):
    return (((x // 2) * 4 + y // 2) * 2) + (z // 2) % 2


def stride_groups(split):
    groups = {}
    for core in range(2):
        for x, y, z in chips():
            half = z // 4
            key = (core, parity(x, y, z)) + ((half,) if split else ())
            order = piece(x, y, z) + (0 if split else 32 * half)
            groups.setdefault(key, []).append((order, device(x, y, z, core)))
    return [[d for _, d in sorted(members)] for members in groups.values()]


def core_pairs():
    return [(device(x, y, z, c), device(x, y, z, 1 - c)) for x, y, z in chips() for c in range(2)]


def home_pairs():
    pairs = []
    for x, y, z in chips():
        for core in range(2):
            to_x = (x & 4) | (core << 1) | ((x >> 1) & 1)
            to_y = (y & 6) | ((z >> 1) & 1)
            to_z = (z & 5) | ((y & 1) << 1)
            pairs.append((device(x, y, z, core), device(to_x, to_y, to_z, x & 1)))
    return pairs


def tokens_kernel(order, grads, features, out):
    for spot in range(8):
        for k in range(2):
            first = pl.multiple_of(order[spot + 8 * k] * 512, 512)
            out[spot, k] = grads[:, pl.ds(first, 512)]
        out[spot, 2] = features[...]


def pack_tokens(order, grads, features):
    vmem = pl.BlockSpec(memory_space=pltpu.VMEM)
    return pl.pallas_call(
        tokens_kernel,
        out_shape=jax.ShapeDtypeStruct((8, 3, 128, 512), jnp.bfloat16),
        in_specs=[pl.BlockSpec(memory_space=pltpu.SMEM), vmem, vmem],
        out_specs=vmem,
        compiler_params=pltpu.CompilerParams(vmem_limit_bytes=32 * MIB),
    )(order, grads, features)


def slots_kernel(live, rows, owner_col, owner_row, deltas, out):
    count = deltas.shape[0]
    before = lax.broadcasted_iota(jnp.int32, (count, count), 0)
    after = lax.broadcasted_iota(jnp.int32, (count, count), 1)
    same = (owner_col[...] == owner_row[...]) & (before < after)
    rank = jnp.sum(same.astype(jnp.float32), axis=0, keepdims=True)
    position = owner_row[...].astype(jnp.float32) * 16.0 + rank
    place = lax.broadcasted_iota(jnp.int32, (256, count), 0).astype(jnp.float32) == position
    place = place.astype(jnp.float32).astype(jnp.bfloat16)
    masked = jnp.where(before < live[0], deltas[...].astype(jnp.float32), 0.0).astype(jnp.bfloat16)
    high, low = rows[...] // 16, rows[...] % 16
    keys = jnp.where(after < 64, high, low).astype(jnp.float32).astype(jnp.bfloat16)
    moved = jnp.dot(place, masked, preferred_element_type=jnp.float32).astype(jnp.bfloat16)
    named = jnp.dot(place, keys, preferred_element_type=jnp.float32).astype(jnp.bfloat16)
    out[:, 0:16, :] = moved.reshape(16, 16, 128)
    out[:, 16:32, :] = named.reshape(16, 16, 128)


def pack_slots(live, rows, owner, deltas):
    vmem = pl.BlockSpec(memory_space=pltpu.VMEM)
    return pl.pallas_call(
        slots_kernel,
        out_shape=jax.ShapeDtypeStruct((16, 32, 128), jnp.bfloat16),
        in_specs=[pl.BlockSpec(memory_space=pltpu.SMEM), vmem, vmem, vmem, vmem],
        out_specs=vmem,
    )(live, rows.reshape(-1, 1), owner, owner.reshape(1, -1), deltas)


def grad_kernel(half, tokens, out):
    first = pl.multiple_of(half[0] * 128, 128)
    second = pl.multiple_of(256 + half[0] * 128, 128)
    left = jnp.concatenate(
        [
            tokens[:, 2, :, pl.ds(first, 128)].reshape(1024, 128),
            tokens[:, 2, :, pl.ds(second, 128)].reshape(1024, 128),
        ],
        axis=1,
    )
    for k in range(2):
        result = lax.dot_general(
            left,
            tokens[:, k, :, :].reshape(1024, 512),
            (((0,), (0,)), ((), ())),
            preferred_element_type=jnp.float32,
        )
        out[k] = result.reshape(2, 128, 512)


def partial_grads(half, tokens):
    return pl.pallas_call(
        grad_kernel,
        out_shape=jax.ShapeDtypeStruct((2, 2, 128, 512), jnp.float32),
        in_specs=[pl.BlockSpec(memory_space=pltpu.SMEM), pl.BlockSpec(memory_space=pltpu.VMEM)],
        out_specs=pl.BlockSpec(memory_space=pltpu.VMEM),
        compiler_params=pltpu.CompilerParams(vmem_limit_bytes=32 * MIB),
        cost_estimate=pl.CostEstimate(flops=1 << 29, bytes_accessed=4 * MIB, transcendentals=0),
    )(half, tokens)


def encode(tiles):
    largest = jnp.abs(tiles[0])
    for tile in tiles[1:]:
        largest = jnp.maximum(largest, jnp.abs(tile))
    largest = jnp.max(jnp.max(largest, axis=1, keepdims=True), axis=2, keepdims=True)
    grade = jnp.ceil(8.0 * jnp.log2(jnp.maximum(largest, 1e-30))) + 1.0
    factor = CODE_RANGE * jnp.exp2(grade * -0.125)
    words, low = [], None
    for t, tile in enumerate(tiles):
        whole = jnp.round(jnp.clip(tile * factor, -CODE_RANGE, CODE_RANGE)).astype(jnp.int32)
        words.append(whole >> 4)
        nibble = (whole & 15) << (4 * t)
        low = nibble if low is None else low | nibble
    spot = lax.broadcasted_iota(jnp.int32, low.shape, 1) + lax.broadcasted_iota(
        jnp.int32, low.shape, 2
    )
    words.append(jnp.where(spot == 0, grade.astype(jnp.int32), low))
    return jnp.concatenate(words, axis=1).astype(jnp.int16)


def decode(words):
    words = words.astype(jnp.int32)
    low = words[:, 32:40, :]
    grade = low[:, 0:1, 0:1].astype(jnp.float32)
    factor = jnp.exp2(grade * 0.125) * (1.0 / CODE_RANGE)
    tiles = []
    for t in range(4):
        whole = words[:, 8 * t : 8 * t + 8, :] * 16 + ((low >> (4 * t)) & 15)
        tiles.append(whole.astype(jnp.float32) * factor)
    return tiles


def share_kernel(kept, arrived, out):
    tiles = []
    for t in range(4):
        cut = slice(t * 128, (t + 1) * 128)
        tiles.append((kept[:, :, :, cut] + arrived[:, :, :, cut]).reshape(64, 8, 128))
    out[...] = encode(tiles)


def share(kept, arrived):
    vmem = pl.BlockSpec(memory_space=pltpu.VMEM)
    return pl.pallas_call(
        share_kernel,
        out_shape=jax.ShapeDtypeStruct((64, 40, 128), jnp.int16),
        in_specs=[vmem, vmem],
        out_specs=vmem,
        compiler_params=pltpu.CompilerParams(vmem_limit_bytes=32 * MIB),
    )(kept, arrived)


def total_kernel(terms, out):
    words = encode([jnp.sum(tile, axis=0, keepdims=True) for tile in decode(terms[...])])
    out[...] = jnp.broadcast_to(words.astype(jnp.int32), (32, 40, 128)).astype(jnp.int16)


def total(terms):
    vmem = pl.BlockSpec(memory_space=pltpu.VMEM)
    return pl.pallas_call(
        total_kernel,
        out_shape=jax.ShapeDtypeStruct((32, 40, 128), jnp.int16),
        in_specs=[vmem],
        out_specs=vmem,
        compiler_params=pltpu.CompilerParams(vmem_limit_bytes=32 * MIB),
    )(terms)


def parts_of(value):
    high = value.astype(jnp.bfloat16)
    return high, (value - high.astype(jnp.float32)).astype(jnp.bfloat16)


def product(a, b, contract):
    return lax.dot_general(a, b, (contract, ((), ())), preferred_element_type=jnp.float32)


def full_product(a, b, contract):
    (ah, al), (bh, bl) = a, b
    return product(ah, bh, contract) + (product(ah, bl, contract) + product(al, bh, contract))


def rows_product(rows, b):
    bh, bl = b
    count = rows.shape[0]
    high, low = parts_of(rows)
    both = jnp.concatenate([high.astype(jnp.float32), low.astype(jnp.float32)], axis=0)
    first = product(both.astype(jnp.bfloat16), bh, ((1,), (0,)))
    return first[:count] + (first[count:] + product(high, bl, ((1,), (0,))))


def direction_kernel(place, own, other, out, grad, power, square):
    half, first_row = place[0], pl.multiple_of(place[1], 8)
    for side, words in ((half, own), (1 - half, other)):
        for t, tile in enumerate(decode(words[...])):
            tile = tile.reshape(2, 128, 128)
            for k in range(2):
                rows = pl.ds(pl.multiple_of(k * 256 + side * 128, 128), 128)
                grad[rows, t * 128 : (t + 1) * 128] = tile[k]
    g = grad[...]
    width = g.shape[0]
    frobenius = jnp.sum(g * g) + 1e-06
    g_parts = parts_of(g)
    normal = full_product(g_parts, g_parts, ((1,), (1,))) / frobenius
    n_parts = parts_of(normal)
    squared = full_product(n_parts, n_parts, ((1,), (0,)))
    total = jnp.sum(jnp.sum(squared * squared, axis=0, keepdims=True), axis=1, keepdims=True)
    bound = jnp.sqrt(jnp.sqrt(total))
    scale = frobenius * bound
    m = normal / bound
    m2 = squared / (bound * bound)
    power[...] = m
    square[...] = m2
    diagonal = lax.broadcasted_iota(jnp.int32, (width, width), 0) == lax.broadcasted_iota(
        jnp.int32, (width, width), 1
    )
    f2 = (jnp.where(diagonal, 25.0, 0.0) - 10.0 * m + m2) / 16.0
    m_parts, f_parts = parts_of(m), parts_of(f2)
    m_rows = power[pl.ds(first_row, 8), :]
    m2_rows = square[pl.ds(first_row, 8), :]
    basis = lax.broadcasted_iota(jnp.int32, (8, width), 1) == first_row + lax.broadcasted_iota(
        jnp.int32, (8, width), 0
    )
    f_rows = (jnp.where(basis, 5.0, 0.0) - m_rows) / 4.0
    fm_rows = (5.0 * m_rows - m2_rows) / 4.0
    root = (5.0 * f_rows - rows_product(rows_product(fm_rows, f_parts), f_parts)) / 4.0
    m_root = rows_product(root, m_parts)
    m2_root = rows_product(m_root, m_parts)
    f_rows = (5.0 * root - m_root) / 4.0
    fm_rows = (5.0 * m_root - m2_root) / 4.0
    root = (5.0 * f_rows - rows_product(rows_product(fm_rows, f_parts), f_parts)) / 4.0
    quarter = 1.0 / jnp.sqrt(jnp.sqrt(scale))
    result = rows_product(root * quarter, g_parts) * quarter * float(width)
    out[...] = result.astype(jnp.bfloat16)


def direction_rows(place, own, other):
    vmem = pl.BlockSpec(memory_space=pltpu.VMEM)
    square = pltpu.VMEM((512, 512), jnp.float32)
    return pl.pallas_call(
        direction_kernel,
        out_shape=jax.ShapeDtypeStruct((8, 512), jnp.bfloat16),
        in_specs=[pl.BlockSpec(memory_space=pltpu.SMEM), vmem, vmem],
        out_specs=vmem,
        scratch_shapes=[square, square, square],
        compiler_params=pltpu.CompilerParams(vmem_limit_bytes=40 * MIB),
    )(place, own, other)


def update_kernel(got, table, accum, new_table, new_accum):
    deltas = got[:, 0:16, :].reshape(256, 128)
    keys = got[:, 16:32, :].astype(jnp.float32).reshape(256, 128)
    row = keys[:, 0:1] * 16.0 + keys[:, 64:65]
    count = table.shape[0]
    named = row == lax.broadcasted_iota(jnp.int32, (256, count), 1).astype(jnp.float32)
    named = named.astype(jnp.float32).astype(jnp.bfloat16)
    summed = lax.dot_general(
        named, deltas, (((0,), (0,)), ((), ())), preferred_element_type=jnp.float32
    )
    before = jnp.transpose(jnp.broadcast_to(accum[...], (128, count)))
    after = before + jnp.sum(summed * summed, axis=1, keepdims=True) / 128.0
    new_table[...] = table[...] - summed / jnp.sqrt(after)
    new_accum[...] = jnp.transpose(after)[0:1, :]


def update_rows(got, table, accum):
    vmem = pl.BlockSpec(memory_space=pltpu.VMEM)
    return pl.pallas_call(
        update_kernel,
        out_shape=(
            jax.ShapeDtypeStruct(table.shape, jnp.float32),
            jax.ShapeDtypeStruct((1, accum.shape[0]), jnp.float32),
        ),
        in_specs=[vmem, vmem, vmem],
        out_specs=(vmem, vmem),
    )(got, table, accum.reshape(1, -1))


def shards(
    features,
    output_grads,
    block_order,
    emb_table,
    row_accum,
    hot_rows,
    hot_owner,
    live_counts,
    hot_deltas,
):
    group, replica = lax.axis_index("grp"), lax.axis_index("rep")
    core, z = group % 2, group // 2
    x, y = replica // SIDE, replica % SIDE
    exchange = partial(lax.all_to_all, split_axis=0, concat_axis=0, tiled=True)

    slots = pack_slots(live_counts, hot_rows, hot_owner, hot_deltas)

    message = pack_tokens(block_order, output_grads, features)
    tokens = exchange(message, AXES, axis_index_groups=cube_groups())
    tokens, slots = lax.optimization_barrier((tokens, slots))

    away = partial_grads((1 - core).reshape(1), tokens)
    arrived = lax.ppermute(away, AXES, core_pairs())
    kept = partial_grads(core.reshape(1), tokens)
    terms = exchange(share(kept, arrived), AXES, axis_index_groups=stride_groups(False))
    own = exchange(total(terms), AXES, axis_index_groups=stride_groups(True))
    got = exchange(slots, "grp")
    other = lax.ppermute(own, AXES, core_pairs())
    turn = piece(x, y, z)
    first_row = (turn // 16) * 256 + core * 128 + (turn % 16) * 8
    rows = direction_rows(jnp.stack([core, first_row]).astype(jnp.int32), own, other)
    home = lax.ppermute(rows, AXES, home_pairs())

    new_table, new_accum = update_rows(got, emb_table, row_accum)
    directions = exchange(jnp.broadcast_to(home[None], (16, 8, 512)), "grp")
    return (new_table, new_accum.reshape(-1), directions)


def solution(mesh):
    return jax.shard_map(
        shards,
        mesh=mesh,
        in_specs=(
            P(AXES, None),
            P(AXES, None),
            P(),
            P(AXES, None),
            P(AXES),
            P(AXES),
            P(AXES, None),
            P(AXES),
            P(AXES, None),
        ),
        out_specs=(P(AXES, None), P(AXES), P(None, "rep", None)),
        check_vma=False,
    )
```

```python
from functools import partial

import jax
import jax.numpy as jnp
from jax import lax
from jax.experimental import pallas as pl
from jax.experimental.pallas import tpu as pltpu
from jax.sharding import PartitionSpec as P

SIDE = 8
AXES = ("grp", "rep")
MIB = 1 << 20
CODE_RANGE = float((1 << 19) - 1)


def device(x, y, z, core):
    return ((z % SIDE) * 2 + core) * (SIDE * SIDE) + (x % SIDE) * SIDE + y % SIDE


def chips():
    for x in range(SIDE):
        for y in range(SIDE):
            for z in range(SIDE):
                yield x, y, z


def parity(x, y, z):
    return (y % 2) * 4 + (z % 2) * 2 + x % 2


def cube_groups():
    groups = []
    for core in range(2):
        for x, y, z in chips():
            if x % 2 != core or y % 2 != core or z % 2 != core:
                continue
            members = [None] * 8
            for dx in range(2):
                for dy in range(2):
                    for dz in range(2):
                        spot = ((x + dx) % SIDE, (y + dy) % SIDE, (z + dz) % SIDE)
                        members[parity(*spot)] = device(*spot, core)
            groups.append(members)
    return groups


def piece(x, y, z):
    return (((x // 2) * 4 + y // 2) * 2) + (z // 2) % 2


def stride_groups(split):
    groups = {}
    for core in range(2):
        for x, y, z in chips():
            half = z // 4
            key = (core, parity(x, y, z)) + ((half,) if split else ())
            order = piece(x, y, z) + (0 if split else 32 * half)
            groups.setdefault(key, []).append((order, device(x, y, z, core)))
    return [[d for _, d in sorted(members)] for members in groups.values()]


def core_pairs():
    return [(device(x, y, z, c), device(x, y, z, 1 - c)) for x, y, z in chips() for c in range(2)]


def home_pairs():
    pairs = []
    for x, y, z in chips():
        for core in range(2):
            to_x = (x & 4) | (core << 1) | ((x >> 1) & 1)
            to_y = (y & 6) | ((z >> 1) & 1)
            to_z = (z & 5) | ((y & 1) << 1)
            pairs.append((device(x, y, z, core), device(to_x, to_y, to_z, x & 1)))
    return pairs


def tokens_kernel(order, grads, features, out):
    for spot in range(8):
        for k in range(2):
            first = pl.multiple_of(order[spot + 8 * k] * 512, 512)
            out[spot, k] = grads[:, pl.ds(first, 512)]
        out[spot, 2] = features[...]


def pack_tokens(order, grads, features):
    vmem = pl.BlockSpec(memory_space=pltpu.VMEM)
    return pl.pallas_call(
        tokens_kernel,
        out_shape=jax.ShapeDtypeStruct((8, 3, 128, 512), jnp.bfloat16),
        in_specs=[pl.BlockSpec(memory_space=pltpu.SMEM), vmem, vmem],
        out_specs=vmem,
        compiler_params=pltpu.CompilerParams(vmem_limit_bytes=60 * MIB),
    )(order, grads, features)


def slots_kernel(live, rows, owner_col, owner_row, deltas, out):
    count = deltas.shape[0]
    before = lax.broadcasted_iota(jnp.int32, (count, count), 0)
    after = lax.broadcasted_iota(jnp.int32, (count, count), 1)
    same = (owner_col[...] == owner_row[...]) & (before < after)
    rank = jnp.sum(same.astype(jnp.float32), axis=0, keepdims=True)
    position = owner_row[...].astype(jnp.float32) * 16.0 + rank
    place = lax.broadcasted_iota(jnp.int32, (256, count), 0).astype(jnp.float32) == position
    place = place.astype(jnp.float32).astype(jnp.bfloat16)
    masked = jnp.where(before < live[0], deltas[...].astype(jnp.float32), 0.0).astype(jnp.bfloat16)
    high, low = rows[...] // 16, rows[...] % 16
    keys = jnp.where(after < 64, high, low).astype(jnp.float32).astype(jnp.bfloat16)
    moved = jnp.dot(place, masked, preferred_element_type=jnp.float32).astype(jnp.bfloat16)
    named = jnp.dot(place, keys, preferred_element_type=jnp.float32).astype(jnp.bfloat16)
    out[:, 0:16, :] = moved.reshape(16, 16, 128)
    out[:, 16:32, :] = named.reshape(16, 16, 128)


def pack_slots(live, rows, owner, deltas):
    vmem = pl.BlockSpec(memory_space=pltpu.VMEM)
    return pl.pallas_call(
        slots_kernel,
        out_shape=jax.ShapeDtypeStruct((16, 32, 128), jnp.bfloat16),
        in_specs=[pl.BlockSpec(memory_space=pltpu.SMEM), vmem, vmem, vmem, vmem],
        out_specs=vmem,
    )(live, rows.reshape(-1, 1), owner, owner.reshape(1, -1), deltas)


def grad_kernel(half, tokens, out):
    first = pl.multiple_of(half[0] * 128, 128)
    second = pl.multiple_of(256 + half[0] * 128, 128)
    left = jnp.concatenate(
        [
            tokens[:, 2, :, pl.ds(first, 128)].reshape(1024, 128),
            tokens[:, 2, :, pl.ds(second, 128)].reshape(1024, 128),
        ],
        axis=1,
    )
    for k in range(2):
        result = lax.dot_general(
            left,
            tokens[:, k, :, :].reshape(1024, 512),
            (((0,), (0,)), ((), ())),
            preferred_element_type=jnp.float32,
        )
        out[k] = result.reshape(2, 128, 512)


def partial_grads(half, tokens):
    return pl.pallas_call(
        grad_kernel,
        out_shape=jax.ShapeDtypeStruct((2, 2, 128, 512), jnp.float32),
        in_specs=[pl.BlockSpec(memory_space=pltpu.SMEM), pl.BlockSpec(memory_space=pltpu.VMEM)],
        out_specs=pl.BlockSpec(memory_space=pltpu.VMEM),
        compiler_params=pltpu.CompilerParams(vmem_limit_bytes=32 * MIB),
        cost_estimate=pl.CostEstimate(flops=1 << 29, bytes_accessed=4 * MIB, transcendentals=0),
    )(half, tokens)


def encode(tiles):
    largest = jnp.abs(tiles[0])
    for tile in tiles[1:]:
        largest = jnp.maximum(largest, jnp.abs(tile))
    largest = jnp.max(jnp.max(largest, axis=1, keepdims=True), axis=2, keepdims=True)
    grade = jnp.ceil(8.0 * jnp.log2(jnp.maximum(largest, 1e-30))) + 1.0
    factor = CODE_RANGE * jnp.exp2(grade * -0.125)
    words, low = [], None
    for t, tile in enumerate(tiles):
        whole = jnp.round(jnp.clip(tile * factor, -CODE_RANGE, CODE_RANGE)).astype(jnp.int32)
        words.append(whole >> 4)
        nibble = (whole & 15) << (4 * t)
        low = nibble if low is None else low | nibble
    spot = lax.broadcasted_iota(jnp.int32, low.shape, 1) + lax.broadcasted_iota(
        jnp.int32, low.shape, 2
    )
    words.append(jnp.where(spot == 0, grade.astype(jnp.int32), low))
    return jnp.concatenate(words, axis=1).astype(jnp.int16)


def decode(words):
    words = words.astype(jnp.int32)
    low = words[:, 32:40, :]
    grade = low[:, 0:1, 0:1].astype(jnp.float32)
    factor = jnp.exp2(grade * 0.125) * (1.0 / CODE_RANGE)
    tiles = []
    for t in range(4):
        whole = words[:, 8 * t : 8 * t + 8, :] * 16 + ((low >> (4 * t)) & 15)
        tiles.append(whole.astype(jnp.float32) * factor)
    return tiles


def share_kernel(kept, arrived, out):
    tiles = []
    for t in range(4):
        cut = slice(t * 128, (t + 1) * 128)
        tiles.append((kept[:, :, :, cut] + arrived[:, :, :, cut]).reshape(64, 8, 128))
    out[...] = encode(tiles)


def share(kept, arrived):
    vmem = pl.BlockSpec(memory_space=pltpu.VMEM)
    return pl.pallas_call(
        share_kernel,
        out_shape=jax.ShapeDtypeStruct((64, 40, 128), jnp.int16),
        in_specs=[vmem, vmem],
        out_specs=vmem,
        compiler_params=pltpu.CompilerParams(vmem_limit_bytes=32 * MIB),
    )(kept, arrived)


def total_kernel(terms, out):
    words = encode([jnp.sum(tile, axis=0, keepdims=True) for tile in decode(terms[...])])
    out[...] = jnp.broadcast_to(words.astype(jnp.int32), (32, 40, 128)).astype(jnp.int16)


def total(terms):
    vmem = pl.BlockSpec(memory_space=pltpu.VMEM)
    return pl.pallas_call(
        total_kernel,
        out_shape=jax.ShapeDtypeStruct((32, 40, 128), jnp.int16),
        in_specs=[vmem],
        out_specs=vmem,
        compiler_params=pltpu.CompilerParams(vmem_limit_bytes=32 * MIB),
    )(terms)


def parts_of(value):
    high = value.astype(jnp.bfloat16)
    return high, (value - high.astype(jnp.float32)).astype(jnp.bfloat16)


def product(a, b, contract):
    return lax.dot_general(a, b, (contract, ((), ())), preferred_element_type=jnp.float32)


def full_product(a, b, contract):
    (ah, al), (bh, bl) = a, b
    return product(ah, bh, contract) + (product(ah, bl, contract) + product(al, bh, contract))


def rows_product(rows, b):
    bh, bl = b
    count = rows.shape[0]
    high, low = parts_of(rows)
    both = jnp.concatenate([high.astype(jnp.float32), low.astype(jnp.float32)], axis=0)
    first = product(both.astype(jnp.bfloat16), bh, ((1,), (0,)))
    return first[:count] + (first[count:] + product(high, bl, ((1,), (0,))))


def direction_kernel(place, own, other, out, grad, power, square):
    half, first_row = place[0], pl.multiple_of(place[1], 8)
    for side, words in ((half, own), (1 - half, other)):
        for t, tile in enumerate(decode(words[...])):
            tile = tile.reshape(2, 128, 128)
            for k in range(2):
                rows = pl.ds(pl.multiple_of(k * 256 + side * 128, 128), 128)
                grad[rows, t * 128 : (t + 1) * 128] = tile[k]
    g = grad[...]
    width = g.shape[0]
    frobenius = jnp.sum(g * g) + 1e-06
    g_parts = parts_of(g)
    normal = full_product(g_parts, g_parts, ((1,), (1,))) / frobenius
    n_parts = parts_of(normal)
    squared = full_product(n_parts, n_parts, ((1,), (0,)))
    total = jnp.sum(jnp.sum(squared * squared, axis=0, keepdims=True), axis=1, keepdims=True)
    bound = jnp.sqrt(jnp.sqrt(total))
    scale = frobenius * bound
    m = normal / bound
    m2 = squared / (bound * bound)
    power[...] = m
    square[...] = m2
    diagonal = lax.broadcasted_iota(jnp.int32, (width, width), 0) == lax.broadcasted_iota(
        jnp.int32, (width, width), 1
    )
    f2 = (jnp.where(diagonal, 25.0, 0.0) - 10.0 * m + m2) / 16.0
    m_parts, f_parts = parts_of(m), parts_of(f2)
    m_rows = power[pl.ds(first_row, 8), :]
    m2_rows = square[pl.ds(first_row, 8), :]
    basis = lax.broadcasted_iota(jnp.int32, (8, width), 1) == first_row + lax.broadcasted_iota(
        jnp.int32, (8, width), 0
    )
    f_rows = (jnp.where(basis, 5.0, 0.0) - m_rows) / 4.0
    fm_rows = (5.0 * m_rows - m2_rows) / 4.0
    root = (5.0 * f_rows - rows_product(rows_product(fm_rows, f_parts), f_parts)) / 4.0
    m_root = rows_product(root, m_parts)
    m2_root = rows_product(m_root, m_parts)
    f_rows = (5.0 * root - m_root) / 4.0
    fm_rows = (5.0 * m_root - m2_root) / 4.0
    root = (5.0 * f_rows - rows_product(rows_product(fm_rows, f_parts), f_parts)) / 4.0
    quarter = 1.0 / jnp.sqrt(jnp.sqrt(scale))
    result = rows_product(root * quarter, g_parts) * quarter * float(width)
    out[...] = result.astype(jnp.bfloat16)


def direction_rows(place, own, other):
    vmem = pl.BlockSpec(memory_space=pltpu.VMEM)
    square = pltpu.VMEM((512, 512), jnp.float32)
    return pl.pallas_call(
        direction_kernel,
        out_shape=jax.ShapeDtypeStruct((8, 512), jnp.bfloat16),
        in_specs=[pl.BlockSpec(memory_space=pltpu.SMEM), vmem, vmem],
        out_specs=vmem,
        scratch_shapes=[square, square, square],
        compiler_params=pltpu.CompilerParams(vmem_limit_bytes=40 * MIB),
    )(place, own, other)


def update_kernel(got, table, accum, new_table, new_accum):
    deltas = got[:, 0:16, :].reshape(256, 128)
    keys = got[:, 16:32, :].astype(jnp.float32).reshape(256, 128)
    row = keys[:, 0:1] * 16.0 + keys[:, 64:65]
    count = table.shape[0]
    named = row == lax.broadcasted_iota(jnp.int32, (256, count), 1).astype(jnp.float32)
    named = named.astype(jnp.float32).astype(jnp.bfloat16)
    summed = lax.dot_general(
        named, deltas, (((0,), (0,)), ((), ())), preferred_element_type=jnp.float32
    )
    before = jnp.transpose(jnp.broadcast_to(accum[...], (128, count)))
    after = before + jnp.sum(summed * summed, axis=1, keepdims=True) / 128.0
    new_table[...] = table[...] - summed / jnp.sqrt(after)
    new_accum[...] = jnp.transpose(after)[0:1, :]


def update_rows(got, table, accum):
    vmem = pl.BlockSpec(memory_space=pltpu.VMEM)
    return pl.pallas_call(
        update_kernel,
        out_shape=(
            jax.ShapeDtypeStruct(table.shape, jnp.float32),
            jax.ShapeDtypeStruct((1, accum.shape[0]), jnp.float32),
        ),
        in_specs=[vmem, vmem, vmem],
        out_specs=(vmem, vmem),
    )(got, table, accum.reshape(1, -1))


def shards(
    features,
    output_grads,
    block_order,
    emb_table,
    row_accum,
    hot_rows,
    hot_owner,
    live_counts,
    hot_deltas,
):
    group, replica = lax.axis_index("grp"), lax.axis_index("rep")
    core, z = group % 2, group // 2
    x, y = replica // SIDE, replica % SIDE
    exchange = partial(lax.all_to_all, split_axis=0, concat_axis=0, tiled=True)

    slots = pack_slots(live_counts, hot_rows, hot_owner, hot_deltas)

    message = pack_tokens(block_order, output_grads, features)
    tokens = exchange(message, AXES, axis_index_groups=cube_groups())
    tokens, slots = lax.optimization_barrier((tokens, slots))

    away = partial_grads((1 - core).reshape(1), tokens)
    arrived = lax.ppermute(away, AXES, core_pairs())
    kept = partial_grads(core.reshape(1), tokens)
    terms = exchange(share(kept, arrived), AXES, axis_index_groups=stride_groups(False))
    own = exchange(total(terms), AXES, axis_index_groups=stride_groups(True))
    got = exchange(slots, "grp")
    other = lax.ppermute(own, AXES, core_pairs())
    turn = piece(x, y, z)
    first_row = (turn // 16) * 256 + core * 128 + (turn % 16) * 8
    rows = direction_rows(jnp.stack([core, first_row]).astype(jnp.int32), own, other)
    home = lax.ppermute(rows, AXES, home_pairs())

    new_table, new_accum = update_rows(got, emb_table, row_accum)
    directions = exchange(jnp.broadcast_to(home[None], (16, 8, 512)), "grp")
    return (new_table, new_accum.reshape(-1), directions)


def solution(mesh):
    return jax.shard_map(
        shards,
        mesh=mesh,
        in_specs=(
            P(AXES, None),
            P(AXES, None),
            P(),
            P(AXES, None),
            P(AXES),
            P(AXES),
            P(AXES, None),
            P(AXES),
            P(AXES, None),
        ),
        out_specs=(P(AXES, None), P(AXES), P(None, "rep", None)),
        check_vma=False,
    )
```

```python
from functools import partial

import jax
import jax.numpy as jnp
from jax import lax
from jax.experimental import pallas as pl
from jax.experimental.pallas import tpu as pltpu
from jax.sharding import PartitionSpec as P

SIDE = 8
AXES = ("grp", "rep")
MIB = 1 << 20
CODE_RANGE = float((1 << 19) - 1)


def device(x, y, z, core):
    return ((z % SIDE) * 2 + core) * (SIDE * SIDE) + (x % SIDE) * SIDE + y % SIDE


def chips():
    for x in range(SIDE):
        for y in range(SIDE):
            for z in range(SIDE):
                yield x, y, z


def parity(x, y, z):
    return (y % 2) * 4 + (z % 2) * 2 + x % 2


def cube_groups():
    groups = []
    for core in range(2):
        for x, y, z in chips():
            if x % 2 != core or y % 2 != core or z % 2 != core:
                continue
            members = [None] * 8
            for dx in range(2):
                for dy in range(2):
                    for dz in range(2):
                        spot = ((x + dx) % SIDE, (y + dy) % SIDE, (z + dz) % SIDE)
                        members[parity(*spot)] = device(*spot, core)
            groups.append(members)
    return groups


def piece(x, y, z):
    return (((x // 2) * 4 + y // 2) * 2) + (z // 2) % 2


def stride_groups(split):
    groups = {}
    for core in range(2):
        for x, y, z in chips():
            half = z // 4
            key = (core, parity(x, y, z)) + ((half,) if split else ())
            order = piece(x, y, z) + (0 if split else 32 * half)
            groups.setdefault(key, []).append((order, device(x, y, z, core)))
    return [[d for _, d in sorted(members)] for members in groups.values()]


def core_pairs():
    return [(device(x, y, z, c), device(x, y, z, 1 - c)) for x, y, z in chips() for c in range(2)]


def z_pairs(step):
    return [(device(x, y, z, c), device(x, y, z ^ step, c)) for x, y, z in chips() for c in range(2)]


def home_pairs():
    pairs = []
    for x, y, z in chips():
        for core in range(2):
            to_x = (x & 4) | (core << 1) | ((x >> 1) & 1)
            to_y = (y & 6) | ((z >> 1) & 1)
            to_z = (z & 5) | ((y & 1) << 1)
            pairs.append((device(x, y, z, core), device(to_x, to_y, to_z, x & 1)))
    return pairs


def tokens_kernel(order, grads, features, out):
    for spot in range(8):
        for k in range(2):
            first = pl.multiple_of(order[spot + 8 * k] * 512, 512)
            out[spot, k] = grads[:, pl.ds(first, 512)]
        out[spot, 2] = features[...]


def pack_tokens(order, grads, features):
    vmem = pl.BlockSpec(memory_space=pltpu.VMEM)
    return pl.pallas_call(
        tokens_kernel,
        out_shape=jax.ShapeDtypeStruct((8, 3, 128, 512), jnp.bfloat16),
        in_specs=[pl.BlockSpec(memory_space=pltpu.SMEM), vmem, vmem],
        out_specs=vmem,
        compiler_params=pltpu.CompilerParams(vmem_limit_bytes=60 * MIB),
    )(order, grads, features)


def slots_kernel(live, core, rows, owner_col, owner_row, deltas, away, kept, placed):
    count = deltas.shape[0]
    before = lax.broadcasted_iota(jnp.int32, (count, count), 0)
    after = lax.broadcasted_iota(jnp.int32, (count, count), 1)
    same = (owner_col[...] == owner_row[...]) & (before < after)
    rank = jnp.sum(same.astype(jnp.float32), axis=0, keepdims=True)
    owner = owner_row[...]
    position = ((owner % 2) * 128 + (owner // 2) * 16).astype(jnp.float32) + rank
    place = lax.broadcasted_iota(jnp.int32, (256, count), 0).astype(jnp.float32) == position
    place = place.astype(jnp.float32).astype(jnp.bfloat16)
    masked = jnp.where(before < live[0], deltas[...].astype(jnp.float32), 0.0).astype(jnp.bfloat16)
    high, low = rows[...] // 16, rows[...] % 16
    keys = jnp.where(after < 64, high, low).astype(jnp.float32).astype(jnp.bfloat16)
    moved = jnp.dot(place, masked, preferred_element_type=jnp.float32).astype(jnp.bfloat16)
    named = jnp.dot(place, keys, preferred_element_type=jnp.float32).astype(jnp.bfloat16)
    placed[:, :, 0:16, :] = moved.reshape(2, 8, 16, 128)
    placed[:, :, 16:32, :] = named.reshape(2, 8, 16, 128)
    away[...] = placed[1 - core[0]]
    kept[...] = placed[core[0]]


def pack_slots(live, core, rows, owner, deltas):
    vmem = pl.BlockSpec(memory_space=pltpu.VMEM)
    smem = pl.BlockSpec(memory_space=pltpu.SMEM)
    half = jax.ShapeDtypeStruct((8, 32, 128), jnp.bfloat16)
    return pl.pallas_call(
        slots_kernel,
        out_shape=(half, half),
        in_specs=[smem, smem, vmem, vmem, vmem, vmem],
        out_specs=(vmem, vmem),
        scratch_shapes=[pltpu.VMEM((2, 8, 32, 128), jnp.bfloat16)],
    )(live, core, rows.reshape(-1, 1), owner, owner.reshape(1, -1), deltas)


def sort_kernel(bit, first, second, away, kept):
    count = first.shape[0]
    for n, source in enumerate((first, second)):
        rows = pl.ds(n * count, count)
        away[rows] = source[:, 1 - bit[0]]
        kept[rows] = source[:, bit[0]]


def sort_slots(bit, first, second, count):
    vmem = pl.BlockSpec(memory_space=pltpu.VMEM)
    split = (count, 2, 4 // count, 32, 128)
    half = jax.ShapeDtypeStruct((2 * count, 4 // count, 32, 128), jnp.bfloat16)
    return pl.pallas_call(
        sort_kernel,
        out_shape=(half, half),
        in_specs=[pl.BlockSpec(memory_space=pltpu.SMEM), vmem, vmem],
        out_specs=(vmem, vmem),
    )(bit, first.reshape(split), second.reshape(split))


def grad_kernel(half, tokens, out):
    first = pl.multiple_of(half[0] * 128, 128)
    second = pl.multiple_of(256 + half[0] * 128, 128)
    left = jnp.concatenate(
        [
            tokens[:, 2, :, pl.ds(first, 128)].reshape(1024, 128),
            tokens[:, 2, :, pl.ds(second, 128)].reshape(1024, 128),
        ],
        axis=1,
    )
    for k in range(2):
        result = lax.dot_general(
            left,
            tokens[:, k, :, :].reshape(1024, 512),
            (((0,), (0,)), ((), ())),
            preferred_element_type=jnp.float32,
        )
        out[k] = result.reshape(2, 128, 512)


def partial_grads(half, tokens):
    return pl.pallas_call(
        grad_kernel,
        out_shape=jax.ShapeDtypeStruct((2, 2, 128, 512), jnp.float32),
        in_specs=[pl.BlockSpec(memory_space=pltpu.SMEM), pl.BlockSpec(memory_space=pltpu.VMEM)],
        out_specs=pl.BlockSpec(memory_space=pltpu.VMEM),
        compiler_params=pltpu.CompilerParams(vmem_limit_bytes=32 * MIB),
        cost_estimate=pl.CostEstimate(flops=1 << 29, bytes_accessed=4 * MIB, transcendentals=0),
    )(half, tokens)


def encode(tiles):
    largest = jnp.abs(tiles[0])
    for tile in tiles[1:]:
        largest = jnp.maximum(largest, jnp.abs(tile))
    largest = jnp.max(jnp.max(largest, axis=1, keepdims=True), axis=2, keepdims=True)
    grade = jnp.ceil(8.0 * jnp.log2(jnp.maximum(largest, 1e-30))) + 1.0
    factor = CODE_RANGE * jnp.exp2(grade * -0.125)
    words, low = [], None
    for t, tile in enumerate(tiles):
        whole = jnp.round(jnp.clip(tile * factor, -CODE_RANGE, CODE_RANGE)).astype(jnp.int32)
        words.append(whole >> 4)
        nibble = (whole & 15) << (4 * t)
        low = nibble if low is None else low | nibble
    spot = lax.broadcasted_iota(jnp.int32, low.shape, 1) + lax.broadcasted_iota(
        jnp.int32, low.shape, 2
    )
    words.append(jnp.where(spot == 0, grade.astype(jnp.int32), low))
    return jnp.concatenate(words, axis=1).astype(jnp.int16)


def decode(words):
    words = words.astype(jnp.int32)
    low = words[:, 32:40, :]
    grade = low[:, 0:1, 0:1].astype(jnp.float32)
    factor = jnp.exp2(grade * 0.125) * (1.0 / CODE_RANGE)
    tiles = []
    for t in range(4):
        whole = words[:, 8 * t : 8 * t + 8, :] * 16 + ((low >> (4 * t)) & 15)
        tiles.append(whole.astype(jnp.float32) * factor)
    return tiles


def share_kernel(kept, arrived, out):
    tiles = []
    for t in range(4):
        cut = slice(t * 128, (t + 1) * 128)
        tiles.append((kept[:, :, :, cut] + arrived[:, :, :, cut]).reshape(64, 8, 128))
    out[...] = encode(tiles)


def share(kept, arrived):
    vmem = pl.BlockSpec(memory_space=pltpu.VMEM)
    return pl.pallas_call(
        share_kernel,
        out_shape=jax.ShapeDtypeStruct((64, 40, 128), jnp.int16),
        in_specs=[vmem, vmem],
        out_specs=vmem,
        compiler_params=pltpu.CompilerParams(vmem_limit_bytes=32 * MIB),
    )(kept, arrived)


def total_kernel(terms, out):
    words = encode([jnp.sum(tile, axis=0, keepdims=True) for tile in decode(terms[...])])
    out[...] = jnp.broadcast_to(words.astype(jnp.int32), (32, 40, 128)).astype(jnp.int16)


def total(terms):
    vmem = pl.BlockSpec(memory_space=pltpu.VMEM)
    return pl.pallas_call(
        total_kernel,
        out_shape=jax.ShapeDtypeStruct((32, 40, 128), jnp.int16),
        in_specs=[vmem],
        out_specs=vmem,
        compiler_params=pltpu.CompilerParams(vmem_limit_bytes=32 * MIB),
    )(terms)


def parts_of(value):
    high = value.astype(jnp.bfloat16)
    return high, (value - high.astype(jnp.float32)).astype(jnp.bfloat16)


def product(a, b, contract):
    return lax.dot_general(a, b, (contract, ((), ())), preferred_element_type=jnp.float32)


def symmetric_product(high, low, contract):
    side = product(high, low, contract)
    return product(high, high, contract) + (side + jnp.transpose(side))


def rows_product(rows, b):
    bh, bl = b
    count = rows.shape[0]
    high, low = parts_of(rows)
    both = jnp.concatenate([high.astype(jnp.float32), low.astype(jnp.float32)], axis=0)
    first = product(both.astype(jnp.bfloat16), bh, ((1,), (0,)))
    return first[:count] + (first[count:] + product(high, bl, ((1,), (0,))))


def direction_kernel(place, own, other, out, grad, power, square):
    half, first_row = place[0], pl.multiple_of(place[1], 8)
    for side, words in ((half, own), (1 - half, other)):
        for t, tile in enumerate(decode(words[...])):
            tile = tile.reshape(2, 128, 128)
            for k in range(2):
                rows = pl.ds(pl.multiple_of(k * 256 + side * 128, 128), 128)
                grad[rows, t * 128 : (t + 1) * 128] = tile[k]
    g = grad[...]
    width = g.shape[0]
    frobenius = jnp.sum(g * g) + 1e-06
    g_parts = parts_of(g)
    normal = symmetric_product(*g_parts, ((1,), (1,))) * (1.0 / frobenius)
    n_parts = parts_of(normal)
    squared = symmetric_product(*n_parts, ((1,), (1,)))
    total = jnp.sum(jnp.sum(squared * squared, axis=0, keepdims=True), axis=1, keepdims=True)
    bound = jnp.sqrt(jnp.sqrt(total))
    scale = frobenius * bound
    to_m = 1.0 / bound
    to_m2 = to_m * to_m
    power[...] = normal
    square[...] = squared
    diagonal = lax.broadcasted_iota(jnp.int32, (width, width), 0) == lax.broadcasted_iota(
        jnp.int32, (width, width), 1
    )
    f2 = jnp.where(diagonal, 25.0 / 16.0, 0.0) + (
        normal * (to_m * (-10.0 / 16.0)) + squared * (to_m2 / 16.0)
    )
    f_parts = parts_of(f2)
    m_rows = power[pl.ds(first_row, 8), :] * to_m
    m2_rows = square[pl.ds(first_row, 8), :] * to_m2
    basis = lax.broadcasted_iota(jnp.int32, (8, width), 1) == first_row + lax.broadcasted_iota(
        jnp.int32, (8, width), 0
    )
    f_rows = (jnp.where(basis, 5.0, 0.0) - m_rows) / 4.0
    fm_rows = (5.0 * m_rows - m2_rows) / 4.0
    root = (5.0 * f_rows - rows_product(rows_product(fm_rows, f_parts), f_parts)) / 4.0
    m_root = rows_product(root, n_parts) * to_m
    m2_root = rows_product(m_root, n_parts) * to_m
    f_rows = (5.0 * root - m_root) / 4.0
    fm_rows = (5.0 * m_root - m2_root) / 4.0
    root = (5.0 * f_rows - rows_product(rows_product(fm_rows, f_parts), f_parts)) / 4.0
    quarter = 1.0 / jnp.sqrt(jnp.sqrt(scale))
    result = rows_product(root * quarter, g_parts) * quarter * float(width)
    out[...] = result.astype(jnp.bfloat16)


def direction_rows(place, own, other):
    vmem = pl.BlockSpec(memory_space=pltpu.VMEM)
    square = pltpu.VMEM((512, 512), jnp.float32)
    return pl.pallas_call(
        direction_kernel,
        out_shape=jax.ShapeDtypeStruct((8, 512), jnp.bfloat16),
        in_specs=[pl.BlockSpec(memory_space=pltpu.SMEM), vmem, vmem],
        out_specs=vmem,
        scratch_shapes=[square, square, square],
        compiler_params=pltpu.CompilerParams(vmem_limit_bytes=40 * MIB),
    )(place, own, other)


def update_kernel(first, second, table, accum, new_table, new_accum):
    deltas = jnp.concatenate(
        [got[:, 0:16, :].reshape(128, 128) for got in (first, second)], axis=0
    )
    keys = jnp.concatenate(
        [got[:, 16:32, :].astype(jnp.float32).reshape(128, 128) for got in (first, second)], axis=0
    )
    row = keys[:, 0:1] * 16.0 + keys[:, 64:65]
    count = table.shape[0]
    named = row == lax.broadcasted_iota(jnp.int32, (256, count), 1).astype(jnp.float32)
    named = named.astype(jnp.float32).astype(jnp.bfloat16)
    summed = lax.dot_general(
        named, deltas, (((0,), (0,)), ((), ())), preferred_element_type=jnp.float32
    )
    before = jnp.transpose(jnp.broadcast_to(accum[...], (128, count)))
    after = before + jnp.sum(summed * summed, axis=1, keepdims=True) / 128.0
    new_table[...] = table[...] - summed / jnp.sqrt(after)
    new_accum[...] = jnp.transpose(after)[0:1, :]


def update_rows(first, second, table, accum):
    vmem = pl.BlockSpec(memory_space=pltpu.VMEM)
    return pl.pallas_call(
        update_kernel,
        out_shape=(
            jax.ShapeDtypeStruct(table.shape, jnp.float32),
            jax.ShapeDtypeStruct((1, accum.shape[0]), jnp.float32),
        ),
        in_specs=[vmem, vmem, vmem, vmem],
        out_specs=(vmem, vmem),
    )(first, second, table, accum.reshape(1, -1))


def shards(
    features,
    output_grads,
    block_order,
    emb_table,
    row_accum,
    hot_rows,
    hot_owner,
    live_counts,
    hot_deltas,
):
    group, replica = lax.axis_index("grp"), lax.axis_index("rep")
    core, z = group % 2, group // 2
    x, y = replica // SIDE, replica % SIDE
    exchange = partial(lax.all_to_all, split_axis=0, concat_axis=0, tiled=True)

    message = pack_tokens(block_order, output_grads, features)
    tokens = exchange(message, AXES, axis_index_groups=cube_groups())

    parting, first = pack_slots(live_counts, core.reshape(1), hot_rows, hot_owner, hot_deltas)
    tokens, parting, first = lax.optimization_barrier((tokens, parting, first))

    away = partial_grads((1 - core).reshape(1), tokens)
    arrived = lax.ppermute(away, AXES, core_pairs())
    kept = partial_grads(core.reshape(1), tokens)
    terms = exchange(share(kept, arrived), AXES, axis_index_groups=stride_groups(False))

    second = lax.ppermute(parting, AXES, core_pairs())
    for step, count in ((4, 1), (2, 2), (1, 4)):
        bit = ((z // step) % 2).reshape(1)
        parting, first = sort_slots(bit, first, second, count)
        second = lax.ppermute(parting, AXES, z_pairs(step))
    first, second = first.reshape(8, 32, 128), second.reshape(8, 32, 128)
    terms, first, second = lax.optimization_barrier((terms, first, second))

    own = exchange(total(terms), AXES, axis_index_groups=stride_groups(True))
    other = lax.ppermute(own, AXES, core_pairs())
    turn = piece(x, y, z)
    first_row = (turn // 16) * 256 + core * 128 + (turn % 16) * 8
    rows = direction_rows(jnp.stack([core, first_row]).astype(jnp.int32), own, other)
    home = lax.ppermute(rows, AXES, home_pairs())

    new_table, new_accum = update_rows(first, second, emb_table, row_accum)
    directions = exchange(jnp.broadcast_to(home[None], (16, 8, 512)), "grp")
    return (new_table, new_accum.reshape(-1), directions)


def solution(mesh):
    return jax.shard_map(
        shards,
        mesh=mesh,
        in_specs=(
            P(AXES, None),
            P(AXES, None),
            P(),
            P(AXES, None),
            P(AXES),
            P(AXES),
            P(AXES, None),
            P(AXES),
            P(AXES, None),
        ),
        out_specs=(P(AXES, None), P(AXES), P(None, "rep", None)),
        check_vma=False,
    )
```

```python
from functools import partial

import jax
import jax.numpy as jnp
from jax import lax
from jax.experimental import pallas as pl
from jax.experimental.pallas import tpu as pltpu
from jax.sharding import PartitionSpec as P

SIDE = 8
AXES = ("grp", "rep")
MIB = 1 << 20
CODE_RANGE = float((1 << 19) - 1)


def device(x, y, z, core):
    return ((z % SIDE) * 2 + core) * (SIDE * SIDE) + (x % SIDE) * SIDE + y % SIDE


def chips():
    for x in range(SIDE):
        for y in range(SIDE):
            for z in range(SIDE):
                yield x, y, z


def parity(x, y, z):
    return (1 - y % 2) * 4 + (z % 2) * 2 + x % 2


def cube_groups():
    groups = []
    for core in range(2):
        for x, y, z in chips():
            if x % 2 != core or y % 2 != core or z % 2 != core:
                continue
            members = [None] * 8
            for dx in range(2):
                for dy in range(2):
                    for dz in range(2):
                        spot = ((x + dx) % SIDE, (y + dy) % SIDE, (z + dz) % SIDE)
                        members[parity(*spot)] = device(*spot, core)
            groups.append(members)
    return groups


def piece(x, y, z):
    return (((x // 2) * 4 + y // 2) * 2) + (z // 2) % 2


def stride_groups(split):
    groups = {}
    for core in range(2):
        for x, y, z in chips():
            half = z // 4
            key = (core, parity(x, y, z)) + ((half,) if split else ())
            order = piece(x, y, z) + (0 if split else 32 * half)
            groups.setdefault(key, []).append((order, device(x, y, z, core)))
    return [[d for _, d in sorted(members)] for members in groups.values()]


def core_pairs():
    return [(device(x, y, z, c), device(x, y, z, 1 - c)) for x, y, z in chips() for c in range(2)]


def home_pairs():
    pairs = []
    for x, y, z in chips():
        for core in range(2):
            to_x = (x & 4) | (core << 1) | ((x >> 1) & 1)
            to_y = (y & 6) | ((z >> 1) & 1)
            to_z = (z & 5) | ((1 - (y & 1)) << 1)
            pairs.append((device(x, y, z, core), device(to_x, to_y, to_z, x & 1)))
    return pairs


def tokens_kernel(order, grads, features, out):
    for spot in range(8):
        for k in range(2):
            first = pl.multiple_of(order[spot + 8 * k] * 512, 512)
            out[spot, k] = grads[:, pl.ds(first, 512)]
        out[spot, 2] = features[...]


def pack_tokens(order, grads, features):
    vmem = pl.BlockSpec(memory_space=pltpu.VMEM)
    return pl.pallas_call(
        tokens_kernel,
        out_shape=jax.ShapeDtypeStruct((8, 3, 128, 512), jnp.bfloat16),
        in_specs=[pl.BlockSpec(memory_space=pltpu.SMEM), vmem, vmem],
        out_specs=vmem,
        compiler_params=pltpu.CompilerParams(vmem_limit_bytes=60 * MIB),
    )(order, grads, features)


def slots_kernel(live, rows, owner_col, owner_row, deltas, out):
    count = deltas.shape[0]
    before = lax.broadcasted_iota(jnp.int32, (count, count), 0)
    after = lax.broadcasted_iota(jnp.int32, (count, count), 1)
    same = (owner_col[...] == owner_row[...]) & (before < after)
    rank = jnp.sum(same.astype(jnp.float32), axis=0, keepdims=True)
    position = owner_row[...].astype(jnp.float32) * 16.0 + rank
    place = lax.broadcasted_iota(jnp.int32, (256, count), 0).astype(jnp.float32) == position
    place = place.astype(jnp.float32).astype(jnp.bfloat16)
    masked = jnp.where(before < live[0], deltas[...].astype(jnp.float32), 0.0).astype(jnp.bfloat16)
    high, low = rows[...] // 16, rows[...] % 16
    keys = jnp.where(after < 64, high, low).astype(jnp.float32).astype(jnp.bfloat16)
    moved = jnp.dot(place, masked, preferred_element_type=jnp.float32).astype(jnp.bfloat16)
    named = jnp.dot(place, keys, preferred_element_type=jnp.float32).astype(jnp.bfloat16)
    out[:, 0:16, :] = moved.reshape(16, 16, 128)
    out[:, 16:32, :] = named.reshape(16, 16, 128)


def pack_slots(live, rows, owner, deltas):
    vmem = pl.BlockSpec(memory_space=pltpu.VMEM)
    return pl.pallas_call(
        slots_kernel,
        out_shape=jax.ShapeDtypeStruct((16, 32, 128), jnp.bfloat16),
        in_specs=[pl.BlockSpec(memory_space=pltpu.SMEM), vmem, vmem, vmem, vmem],
        out_specs=vmem,
    )(live, rows.reshape(-1, 1), owner, owner.reshape(1, -1), deltas)


def grad_kernel(half, tokens, out):
    first = pl.multiple_of(half[0] * 128, 128)
    second = pl.multiple_of(256 + half[0] * 128, 128)
    left = jnp.concatenate(
        [
            tokens[:, 2, :, pl.ds(first, 128)].reshape(1024, 128),
            tokens[:, 2, :, pl.ds(second, 128)].reshape(1024, 128),
        ],
        axis=1,
    )
    for k in range(2):
        result = lax.dot_general(
            left,
            tokens[:, k, :, :].reshape(1024, 512),
            (((0,), (0,)), ((), ())),
            preferred_element_type=jnp.float32,
        )
        out[k] = result.reshape(2, 128, 512)


def partial_grads(half, tokens):
    return pl.pallas_call(
        grad_kernel,
        out_shape=jax.ShapeDtypeStruct((2, 2, 128, 512), jnp.float32),
        in_specs=[pl.BlockSpec(memory_space=pltpu.SMEM), pl.BlockSpec(memory_space=pltpu.VMEM)],
        out_specs=pl.BlockSpec(memory_space=pltpu.VMEM),
        compiler_params=pltpu.CompilerParams(vmem_limit_bytes=32 * MIB),
        cost_estimate=pl.CostEstimate(flops=1 << 29, bytes_accessed=4 * MIB, transcendentals=0),
    )(half, tokens)


def encode(tiles):
    largest = jnp.abs(tiles[0])
    for tile in tiles[1:]:
        largest = jnp.maximum(largest, jnp.abs(tile))
    largest = jnp.max(jnp.max(largest, axis=1, keepdims=True), axis=2, keepdims=True)
    grade = jnp.ceil(8.0 * jnp.log2(jnp.maximum(largest, 1e-30))) + 1.0
    factor = CODE_RANGE * jnp.exp2(grade * -0.125)
    words, low = [], None
    for t, tile in enumerate(tiles):
        whole = jnp.round(jnp.clip(tile * factor, -CODE_RANGE, CODE_RANGE)).astype(jnp.int32)
        words.append(whole >> 4)
        nibble = (whole & 15) << (4 * t)
        low = nibble if low is None else low | nibble
    spot = lax.broadcasted_iota(jnp.int32, low.shape, 1) + lax.broadcasted_iota(
        jnp.int32, low.shape, 2
    )
    words.append(jnp.where(spot == 0, grade.astype(jnp.int32), low))
    return jnp.concatenate(words, axis=1).astype(jnp.int16)


def decode(words):
    words = words.astype(jnp.int32)
    low = words[:, 32:40, :]
    grade = low[:, 0:1, 0:1].astype(jnp.float32)
    factor = jnp.exp2(grade * 0.125) * (1.0 / CODE_RANGE)
    tiles = []
    for t in range(4):
        whole = words[:, 8 * t : 8 * t + 8, :] * 16 + ((low >> (4 * t)) & 15)
        tiles.append(whole.astype(jnp.float32) * factor)
    return tiles


def share_kernel(kept, arrived, out):
    tiles = []
    for t in range(4):
        cut = slice(t * 128, (t + 1) * 128)
        tiles.append((kept[:, :, :, cut] + arrived[:, :, :, cut]).reshape(64, 8, 128))
    out[...] = encode(tiles)


def share(kept, arrived):
    vmem = pl.BlockSpec(memory_space=pltpu.VMEM)
    return pl.pallas_call(
        share_kernel,
        out_shape=jax.ShapeDtypeStruct((64, 40, 128), jnp.int16),
        in_specs=[vmem, vmem],
        out_specs=vmem,
        compiler_params=pltpu.CompilerParams(vmem_limit_bytes=32 * MIB),
    )(kept, arrived)


def total_kernel(terms, out):
    words = encode([jnp.sum(tile, axis=0, keepdims=True) for tile in decode(terms[...])])
    out[...] = jnp.broadcast_to(words.astype(jnp.int32), (32, 40, 128)).astype(jnp.int16)


def total(terms):
    vmem = pl.BlockSpec(memory_space=pltpu.VMEM)
    return pl.pallas_call(
        total_kernel,
        out_shape=jax.ShapeDtypeStruct((32, 40, 128), jnp.int16),
        in_specs=[vmem],
        out_specs=vmem,
        compiler_params=pltpu.CompilerParams(vmem_limit_bytes=32 * MIB),
    )(terms)


def parts_of(value):
    high = value.astype(jnp.bfloat16)
    return high, (value - high.astype(jnp.float32)).astype(jnp.bfloat16)


def product(a, b, contract):
    return lax.dot_general(a, b, (contract, ((), ())), preferred_element_type=jnp.float32)


def symmetric_product(high, low, contract):
    side = product(high, low, contract)
    return product(high, high, contract) + (side + jnp.transpose(side))


def rows_product(rows, b):
    bh, bl = b
    count = rows.shape[0]
    high, low = parts_of(rows)
    both = jnp.concatenate([high.astype(jnp.float32), low.astype(jnp.float32)], axis=0)
    first = product(both.astype(jnp.bfloat16), bh, ((1,), (0,)))
    return first[:count] + (first[count:] + product(high, bl, ((1,), (0,))))


def direction_kernel(place, own, other, out, grad, power, square):
    half, first_row = place[0], pl.multiple_of(place[1], 8)
    for side, words in ((half, own), (1 - half, other)):
        for t, tile in enumerate(decode(words[...])):
            tile = tile.reshape(2, 128, 128)
            for k in range(2):
                rows = pl.ds(pl.multiple_of(k * 256 + side * 128, 128), 128)
                grad[rows, t * 128 : (t + 1) * 128] = tile[k]
    g = grad[...]
    width = g.shape[0]
    frobenius = jnp.sum(g * g) + 1e-06
    g_parts = parts_of(g)
    normal = symmetric_product(*g_parts, ((1,), (1,))) * (1.0 / frobenius)
    n_parts = parts_of(normal)
    squared = symmetric_product(*n_parts, ((1,), (1,)))
    total = jnp.sum(jnp.sum(squared * squared, axis=0, keepdims=True), axis=1, keepdims=True)
    bound = jnp.sqrt(jnp.sqrt(total))
    scale = frobenius * bound
    to_m = 1.0 / bound
    to_m2 = to_m * to_m
    power[...] = normal
    square[...] = squared
    diagonal = lax.broadcasted_iota(jnp.int32, (width, width), 0) == lax.broadcasted_iota(
        jnp.int32, (width, width), 1
    )
    f2 = jnp.where(diagonal, 25.0 / 16.0, 0.0) + (
        normal * (to_m * (-10.0 / 16.0)) + squared * (to_m2 / 16.0)
    )
    f_parts = parts_of(f2)
    m_rows = power[pl.ds(first_row, 8), :] * to_m
    m2_rows = square[pl.ds(first_row, 8), :] * to_m2
    basis = lax.broadcasted_iota(jnp.int32, (8, width), 1) == first_row + lax.broadcasted_iota(
        jnp.int32, (8, width), 0
    )
    f_rows = (jnp.where(basis, 5.0, 0.0) - m_rows) / 4.0
    fm_rows = (5.0 * m_rows - m2_rows) / 4.0
    root = (5.0 * f_rows - rows_product(rows_product(fm_rows, f_parts), f_parts)) / 4.0
    m_root = rows_product(root, n_parts) * to_m
    m2_root = rows_product(m_root, n_parts) * to_m
    f_rows = (5.0 * root - m_root) / 4.0
    fm_rows = (5.0 * m_root - m2_root) / 4.0
    root = (5.0 * f_rows - rows_product(rows_product(fm_rows, f_parts), f_parts)) / 4.0
    quarter = 1.0 / jnp.sqrt(jnp.sqrt(scale))
    result = rows_product(root * quarter, g_parts) * quarter * float(width)
    out[...] = result.astype(jnp.bfloat16)


def direction_rows(place, own, other):
    vmem = pl.BlockSpec(memory_space=pltpu.VMEM)
    square = pltpu.VMEM((512, 512), jnp.float32)
    return pl.pallas_call(
        direction_kernel,
        out_shape=jax.ShapeDtypeStruct((8, 512), jnp.bfloat16),
        in_specs=[pl.BlockSpec(memory_space=pltpu.SMEM), vmem, vmem],
        out_specs=vmem,
        scratch_shapes=[square, square, square],
        compiler_params=pltpu.CompilerParams(vmem_limit_bytes=40 * MIB),
    )(place, own, other)


def update_kernel(got, table, accum, new_table, new_accum):
    deltas = got[:, 0:16, :].reshape(256, 128)
    keys = got[:, 16:32, :].astype(jnp.float32).reshape(256, 128)
    row = keys[:, 0:1] * 16.0 + keys[:, 64:65]
    count = table.shape[0]
    named = row == lax.broadcasted_iota(jnp.int32, (256, count), 1).astype(jnp.float32)
    named = named.astype(jnp.float32).astype(jnp.bfloat16)
    summed = lax.dot_general(
        named, deltas, (((0,), (0,)), ((), ())), preferred_element_type=jnp.float32
    )
    before = jnp.transpose(jnp.broadcast_to(accum[...], (128, count)))
    after = before + jnp.sum(summed * summed, axis=1, keepdims=True) / 128.0
    new_table[...] = table[...] - summed / jnp.sqrt(after)
    new_accum[...] = jnp.transpose(after)[0:1, :]


def update_rows(got, table, accum):
    vmem = pl.BlockSpec(memory_space=pltpu.VMEM)
    return pl.pallas_call(
        update_kernel,
        out_shape=(
            jax.ShapeDtypeStruct(table.shape, jnp.float32),
            jax.ShapeDtypeStruct((1, accum.shape[0]), jnp.float32),
        ),
        in_specs=[vmem, vmem, vmem],
        out_specs=(vmem, vmem),
    )(got, table, accum.reshape(1, -1))


def shards(
    features,
    output_grads,
    block_order,
    emb_table,
    row_accum,
    hot_rows,
    hot_owner,
    live_counts,
    hot_deltas,
):
    group, replica = lax.axis_index("grp"), lax.axis_index("rep")
    core, z = group % 2, group // 2
    x, y = replica // SIDE, replica % SIDE
    exchange = partial(lax.all_to_all, split_axis=0, concat_axis=0, tiled=True)

    slots = pack_slots(live_counts, hot_rows, hot_owner, hot_deltas)

    message = pack_tokens(block_order, output_grads, features)
    tokens = exchange(message, AXES, axis_index_groups=cube_groups())
    tokens, slots = lax.optimization_barrier((tokens, slots))

    away = partial_grads((1 - core).reshape(1), tokens)
    arrived = lax.ppermute(away, AXES, core_pairs())
    kept = partial_grads(core.reshape(1), tokens)
    terms = exchange(share(kept, arrived), AXES, axis_index_groups=stride_groups(False))
    own = exchange(total(terms), AXES, axis_index_groups=stride_groups(True))
    got = exchange(slots, "grp")
    other = lax.ppermute(own, AXES, core_pairs())
    turn = piece(x, y, z)
    first_row = (turn // 16) * 256 + core * 128 + (turn % 16) * 8
    rows = direction_rows(jnp.stack([core, first_row]).astype(jnp.int32), own, other)
    home = lax.ppermute(rows, AXES, home_pairs())

    new_table, new_accum = update_rows(got, emb_table, row_accum)
    directions = exchange(jnp.broadcast_to(home[None], (16, 8, 512)), "grp")
    return (new_table, new_accum.reshape(-1), directions)


def solution(mesh):
    return jax.shard_map(
        shards,
        mesh=mesh,
        in_specs=(
            P(AXES, None),
            P(AXES, None),
            P(),
            P(AXES, None),
            P(AXES),
            P(AXES),
            P(AXES, None),
            P(AXES),
            P(AXES, None),
        ),
        out_specs=(P(AXES, None), P(AXES), P(None, "rep", None)),
        check_vma=False,
    )
```

```python
from functools import partial

import jax
import jax.numpy as jnp
from jax import lax
from jax.experimental import pallas as pl
from jax.experimental.pallas import tpu as pltpu
from jax.sharding import PartitionSpec as P

SIDE = 8
AXES = ("grp", "rep")
MIB = 1 << 20
CODE_RANGE = float((1 << 19) - 1)


def device(x, y, z, core):
    return ((z % SIDE) * 2 + core) * (SIDE * SIDE) + (x % SIDE) * SIDE + y % SIDE


def chips():
    for x in range(SIDE):
        for y in range(SIDE):
            for z in range(SIDE):
                yield x, y, z


def parity(x, y, z):
    return (1 - y % 2) * 4 + (z % 2) * 2 + x % 2


def cube_groups():
    groups = []
    for core in range(2):
        for x, y, z in chips():
            if x % 2 != core or y % 2 != core or z % 2 != core:
                continue
            members = [None] * 8
            for dx in range(2):
                for dy in range(2):
                    for dz in range(2):
                        spot = ((x + dx) % SIDE, (y + dy) % SIDE, (z + dz) % SIDE)
                        members[parity(*spot)] = device(*spot, core)
            groups.append(members)
    return groups


def piece(x, y, z):
    return (((x // 2) * 4 + y // 2) * 2) + (z // 2) % 2


def stride_groups(split):
    groups = {}
    for core in range(2):
        for x, y, z in chips():
            half = z // 4
            key = (core, parity(x, y, z)) + ((half,) if split else ())
            order = piece(x, y, z) + (0 if split else 32 * half)
            groups.setdefault(key, []).append((order, device(x, y, z, core)))
    return [[d for _, d in sorted(members)] for members in groups.values()]


def core_pairs():
    return [(device(x, y, z, c), device(x, y, z, 1 - c)) for x, y, z in chips() for c in range(2)]


def home_pairs():
    pairs = []
    for x, y, z in chips():
        for core in range(2):
            to_x = (x & 4) | (core << 1) | ((x >> 1) & 1)
            to_y = (y & 6) | ((z >> 1) & 1)
            to_z = (z & 5) | ((1 - (y & 1)) << 1)
            pairs.append((device(x, y, z, core), device(to_x, to_y, to_z, x & 1)))
    return pairs


def tokens_kernel(order, grads, features, out):
    for spot in range(8):
        for k in range(2):
            first = pl.multiple_of(order[spot + 8 * k] * 512, 512)
            out[spot, k] = grads[:, pl.ds(first, 512)]
        out[spot, 2] = features[...]


def pack_tokens(order, grads, features):
    vmem = pl.BlockSpec(memory_space=pltpu.VMEM)
    return pl.pallas_call(
        tokens_kernel,
        out_shape=jax.ShapeDtypeStruct((8, 3, 128, 512), jnp.bfloat16),
        in_specs=[pl.BlockSpec(memory_space=pltpu.SMEM), vmem, vmem],
        out_specs=vmem,
        compiler_params=pltpu.CompilerParams(vmem_limit_bytes=60 * MIB),
    )(order, grads, features)


def slots_kernel(live, rows, owner_col, owner_row, deltas, out):
    count = deltas.shape[0]
    before = lax.broadcasted_iota(jnp.int32, (count, count), 0)
    after = lax.broadcasted_iota(jnp.int32, (count, count), 1)
    same = (owner_col[...] == owner_row[...]) & (before < after)
    rank = jnp.sum(same.astype(jnp.float32), axis=0, keepdims=True)
    position = owner_row[...].astype(jnp.float32) * 16.0 + rank
    place = lax.broadcasted_iota(jnp.int32, (256, count), 0).astype(jnp.float32) == position
    place = place.astype(jnp.float32).astype(jnp.bfloat16)
    masked = jnp.where(before < live[0], deltas[...].astype(jnp.float32), 0.0).astype(jnp.bfloat16)
    high, low = rows[...] // 16, rows[...] % 16
    keys = jnp.where(after < 64, high, low).astype(jnp.float32).astype(jnp.bfloat16)
    moved = jnp.dot(place, masked, preferred_element_type=jnp.float32).astype(jnp.bfloat16)
    named = jnp.dot(place, keys, preferred_element_type=jnp.float32).astype(jnp.bfloat16)
    out[:, 0:16, :] = moved.reshape(16, 16, 128)
    out[:, 16:32, :] = named.reshape(16, 16, 128)


def pack_slots(live, rows, owner, deltas):
    vmem = pl.BlockSpec(memory_space=pltpu.VMEM)
    return pl.pallas_call(
        slots_kernel,
        out_shape=jax.ShapeDtypeStruct((16, 32, 128), jnp.bfloat16),
        in_specs=[pl.BlockSpec(memory_space=pltpu.SMEM), vmem, vmem, vmem, vmem],
        out_specs=vmem,
    )(live, rows.reshape(-1, 1), owner, owner.reshape(1, -1), deltas)


def grad_kernel(half, tokens, out):
    first = pl.multiple_of(half[0] * 128, 128)
    second = pl.multiple_of(256 + half[0] * 128, 128)
    left = jnp.concatenate(
        [
            tokens[:, 2, :, pl.ds(first, 128)].reshape(1024, 128),
            tokens[:, 2, :, pl.ds(second, 128)].reshape(1024, 128),
        ],
        axis=1,
    )
    for k in range(2):
        result = lax.dot_general(
            left,
            tokens[:, k, :, :].reshape(1024, 512),
            (((0,), (0,)), ((), ())),
            preferred_element_type=jnp.float32,
        )
        out[k] = result.reshape(2, 128, 512)


def partial_grads(half, tokens):
    return pl.pallas_call(
        grad_kernel,
        out_shape=jax.ShapeDtypeStruct((2, 2, 128, 512), jnp.float32),
        in_specs=[pl.BlockSpec(memory_space=pltpu.SMEM), pl.BlockSpec(memory_space=pltpu.VMEM)],
        out_specs=pl.BlockSpec(memory_space=pltpu.VMEM),
        compiler_params=pltpu.CompilerParams(vmem_limit_bytes=32 * MIB),
        cost_estimate=pl.CostEstimate(flops=1 << 29, bytes_accessed=4 * MIB, transcendentals=0),
    )(half, tokens)


def encode(tiles):
    largest = jnp.abs(tiles[0])
    for tile in tiles[1:]:
        largest = jnp.maximum(largest, jnp.abs(tile))
    largest = jnp.max(jnp.max(largest, axis=1, keepdims=True), axis=2, keepdims=True)
    grade = jnp.ceil(8.0 * jnp.log2(jnp.maximum(largest, 1e-30))) + 1.0
    factor = CODE_RANGE * jnp.exp2(grade * -0.125)
    words, low = [], None
    for t, tile in enumerate(tiles):
        whole = jnp.round(jnp.clip(tile * factor, -CODE_RANGE, CODE_RANGE)).astype(jnp.int32)
        words.append(whole >> 4)
        nibble = (whole & 15) << (4 * t)
        low = nibble if low is None else low | nibble
    spot = lax.broadcasted_iota(jnp.int32, low.shape, 1) + lax.broadcasted_iota(
        jnp.int32, low.shape, 2
    )
    words.append(jnp.where(spot == 0, grade.astype(jnp.int32), low))
    return jnp.concatenate(words, axis=1).astype(jnp.int16)


def decode(words):
    words = words.astype(jnp.int32)
    low = words[:, 32:40, :]
    grade = low[:, 0:1, 0:1].astype(jnp.float32)
    factor = jnp.exp2(grade * 0.125) * (1.0 / CODE_RANGE)
    tiles = []
    for t in range(4):
        whole = words[:, 8 * t : 8 * t + 8, :] * 16 + ((low >> (4 * t)) & 15)
        tiles.append(whole.astype(jnp.float32) * factor)
    return tiles


def share_kernel(kept, arrived, out):
    tiles = []
    for t in range(4):
        cut = slice(t * 128, (t + 1) * 128)
        tiles.append((kept[:, :, :, cut] + arrived[:, :, :, cut]).reshape(64, 8, 128))
    out[...] = encode(tiles)


def share(kept, arrived):
    vmem = pl.BlockSpec(memory_space=pltpu.VMEM)
    return pl.pallas_call(
        share_kernel,
        out_shape=jax.ShapeDtypeStruct((64, 40, 128), jnp.int16),
        in_specs=[vmem, vmem],
        out_specs=vmem,
        compiler_params=pltpu.CompilerParams(vmem_limit_bytes=32 * MIB),
    )(kept, arrived)


def total_kernel(terms, out):
    words = encode([jnp.sum(tile, axis=0, keepdims=True) for tile in decode(terms[...])])
    out[...] = jnp.broadcast_to(words.astype(jnp.int32), (32, 40, 128)).astype(jnp.int16)


def total(terms):
    vmem = pl.BlockSpec(memory_space=pltpu.VMEM)
    return pl.pallas_call(
        total_kernel,
        out_shape=jax.ShapeDtypeStruct((32, 40, 128), jnp.int16),
        in_specs=[vmem],
        out_specs=vmem,
        compiler_params=pltpu.CompilerParams(vmem_limit_bytes=32 * MIB),
    )(terms)


def parts_of(value):
    high = value.astype(jnp.bfloat16)
    return high, (value - high.astype(jnp.float32)).astype(jnp.bfloat16)


def product(a, b, contract):
    return lax.dot_general(a, b, (contract, ((), ())), preferred_element_type=jnp.float32)


def symmetric_product(high, low, contract):
    side = product(high, low, contract)
    return product(high, high, contract) + (side + jnp.transpose(side))


def rows_product(rows, b):
    bh, bl = b
    count = rows.shape[0]
    high, low = parts_of(rows)
    both = jnp.concatenate([high.astype(jnp.float32), low.astype(jnp.float32)], axis=0)
    first = product(both.astype(jnp.bfloat16), bh, ((1,), (0,)))
    return first[:count] + (first[count:] + product(high, bl, ((1,), (0,))))


def direction_kernel(place, own, other, out, grad, power, square):
    half, first_row = place[0], pl.multiple_of(place[1], 8)
    for side, words in ((half, own), (1 - half, other)):
        for t, tile in enumerate(decode(words[...])):
            tile = tile.reshape(2, 128, 128)
            for k in range(2):
                rows = pl.ds(pl.multiple_of(k * 256 + side * 128, 128), 128)
                grad[rows, t * 128 : (t + 1) * 128] = tile[k]
    g = grad[...]
    width = g.shape[0]
    frobenius = jnp.sum(g * g) + 1e-06
    g_parts = parts_of(g)
    inverse = 1.0 / jnp.sqrt(frobenius)
    normal = symmetric_product(*g_parts, ((1,), (1,))) * inverse * inverse
    n_parts = parts_of(normal)
    squared = symmetric_product(*n_parts, ((1,), (1,)))
    total = jnp.sum(jnp.sum(squared * squared, axis=0, keepdims=True), axis=1, keepdims=True)
    bound = jnp.sqrt(jnp.sqrt(total))
    scale = frobenius * bound
    to_m = 1.0 / bound
    to_m2 = to_m * to_m
    power[...] = normal
    square[...] = squared
    diagonal = lax.broadcasted_iota(jnp.int32, (width, width), 0) == lax.broadcasted_iota(
        jnp.int32, (width, width), 1
    )
    f2 = jnp.where(diagonal, 25.0 / 16.0, 0.0) + (
        normal * (to_m * (-10.0 / 16.0)) + squared * (to_m2 / 16.0)
    )
    f_parts = parts_of(f2)
    m_rows = power[pl.ds(first_row, 8), :] * to_m
    m2_rows = square[pl.ds(first_row, 8), :] * to_m2
    basis = lax.broadcasted_iota(jnp.int32, (8, width), 1) == first_row + lax.broadcasted_iota(
        jnp.int32, (8, width), 0
    )
    f_rows = (jnp.where(basis, 5.0, 0.0) - m_rows) / 4.0
    fm_rows = (5.0 * m_rows - m2_rows) / 4.0
    root = (5.0 * f_rows - rows_product(rows_product(fm_rows, f_parts), f_parts)) / 4.0
    m_root = rows_product(root, n_parts) * to_m
    m2_root = rows_product(m_root, n_parts) * to_m
    f_rows = (5.0 * root - m_root) / 4.0
    fm_rows = (5.0 * m_root - m2_root) / 4.0
    root = (5.0 * f_rows - rows_product(rows_product(fm_rows, f_parts), f_parts)) / 4.0
    quarter = 1.0 / jnp.sqrt(jnp.sqrt(scale))
    result = rows_product(root * quarter, g_parts) * quarter * float(width)
    out[...] = result.astype(jnp.bfloat16)


def direction_rows(place, own, other):
    vmem = pl.BlockSpec(memory_space=pltpu.VMEM)
    square = pltpu.VMEM((512, 512), jnp.float32)
    return pl.pallas_call(
        direction_kernel,
        out_shape=jax.ShapeDtypeStruct((8, 512), jnp.bfloat16),
        in_specs=[pl.BlockSpec(memory_space=pltpu.SMEM), vmem, vmem],
        out_specs=vmem,
        scratch_shapes=[square, square, square],
        compiler_params=pltpu.CompilerParams(vmem_limit_bytes=40 * MIB),
    )(place, own, other)


def update_kernel(got, table, accum, new_table, new_accum):
    deltas = got[:, 0:16, :].reshape(256, 128)
    keys = got[:, 16:32, :].astype(jnp.float32).reshape(256, 128)
    row = keys[:, 0:1] * 16.0 + keys[:, 64:65]
    count = table.shape[0]
    named = row == lax.broadcasted_iota(jnp.int32, (256, count), 1).astype(jnp.float32)
    named = named.astype(jnp.float32).astype(jnp.bfloat16)
    summed = lax.dot_general(
        named, deltas, (((0,), (0,)), ((), ())), preferred_element_type=jnp.float32
    )
    before = jnp.transpose(jnp.broadcast_to(accum[...], (128, count)))
    after = before + jnp.sum(summed * summed, axis=1, keepdims=True) / 128.0
    new_table[...] = table[...] - summed / jnp.sqrt(after)
    new_accum[...] = jnp.transpose(after)[0:1, :]


def update_rows(got, table, accum):
    vmem = pl.BlockSpec(memory_space=pltpu.VMEM)
    return pl.pallas_call(
        update_kernel,
        out_shape=(
            jax.ShapeDtypeStruct(table.shape, jnp.float32),
            jax.ShapeDtypeStruct((1, accum.shape[0]), jnp.float32),
        ),
        in_specs=[vmem, vmem, vmem],
        out_specs=(vmem, vmem),
    )(got, table, accum.reshape(1, -1))


def shards(
    features,
    output_grads,
    block_order,
    emb_table,
    row_accum,
    hot_rows,
    hot_owner,
    live_counts,
    hot_deltas,
):
    group, replica = lax.axis_index("grp"), lax.axis_index("rep")
    core, z = group % 2, group // 2
    x, y = replica // SIDE, replica % SIDE
    exchange = partial(lax.all_to_all, split_axis=0, concat_axis=0, tiled=True)

    slots = pack_slots(live_counts, hot_rows, hot_owner, hot_deltas)

    message = pack_tokens(block_order, output_grads, features)
    tokens = exchange(message, AXES, axis_index_groups=cube_groups())
    tokens, slots = lax.optimization_barrier((tokens, slots))

    away = partial_grads((1 - core).reshape(1), tokens)
    arrived = lax.ppermute(away, AXES, core_pairs())
    kept = partial_grads(core.reshape(1), tokens)
    terms = exchange(share(kept, arrived), AXES, axis_index_groups=stride_groups(False))
    own = exchange(total(terms), AXES, axis_index_groups=stride_groups(True))
    got = exchange(slots, "grp")
    other = lax.ppermute(own, AXES, core_pairs())
    turn = piece(x, y, z)
    first_row = (turn // 16) * 256 + core * 128 + (turn % 16) * 8
    rows = direction_rows(jnp.stack([core, first_row]).astype(jnp.int32), own, other)
    home = lax.ppermute(rows, AXES, home_pairs())

    new_table, new_accum = update_rows(got, emb_table, row_accum)
    directions = exchange(jnp.broadcast_to(home[None], (16, 8, 512)), "grp")
    return (new_table, new_accum.reshape(-1), directions)


def solution(mesh):
    return jax.shard_map(
        shards,
        mesh=mesh,
        in_specs=(
            P(AXES, None),
            P(AXES, None),
            P(),
            P(AXES, None),
            P(AXES),
            P(AXES),
            P(AXES, None),
            P(AXES),
            P(AXES, None),
        ),
        out_specs=(P(AXES, None), P(AXES), P(None, "rep", None)),
        check_vma=False,
    )
```

```python
from functools import partial

import jax
import jax.numpy as jnp
from jax import lax
from jax.experimental import pallas as pl
from jax.experimental.pallas import tpu as pltpu
from jax.sharding import PartitionSpec as P

SIDE = 8
AXES = ("grp", "rep")
MIB = 1 << 20
CODE_RANGE = float((1 << 19) - 1)


def device(x, y, z, core):
    return ((z % SIDE) * 2 + core) * (SIDE * SIDE) + (x % SIDE) * SIDE + y % SIDE


def chips():
    for x in range(SIDE):
        for y in range(SIDE):
            for z in range(SIDE):
                yield x, y, z


def parity(x, y, z):
    return (1 - y % 2) * 4 + (z % 2) * 2 + x % 2


def cube_groups():
    groups = []
    for core in range(2):
        for x, y, z in chips():
            if x % 2 != core or y % 2 != core or z % 2 != core:
                continue
            members = [None] * 8
            for dx in range(2):
                for dy in range(2):
                    for dz in range(2):
                        spot = ((x + dx) % SIDE, (y + dy) % SIDE, (z + dz) % SIDE)
                        members[parity(*spot)] = device(*spot, core)
            groups.append(members)
    return groups


def piece(x, y, z):
    return (((x // 2) * 4 + y // 2) * 2) + (z // 2) % 2


def stride_groups(split):
    groups = {}
    for core in range(2):
        for x, y, z in chips():
            half = z // 4
            key = (core, parity(x, y, z)) + ((half,) if split else ())
            order = piece(x, y, z) + (0 if split else 32 * half)
            groups.setdefault(key, []).append((order, device(x, y, z, core)))
    return [[d for _, d in sorted(members)] for members in groups.values()]


def core_pairs():
    return [(device(x, y, z, c), device(x, y, z, 1 - c)) for x, y, z in chips() for c in range(2)]


def home_pairs():
    pairs = []
    for x, y, z in chips():
        for core in range(2):
            to_x = (x & 4) | (core << 1) | ((x >> 1) & 1)
            to_y = (y & 6) | ((z >> 1) & 1)
            to_z = (z & 5) | ((1 - (y & 1)) << 1)
            pairs.append((device(x, y, z, core), device(to_x, to_y, to_z, x & 1)))
    return pairs


def tokens_kernel(order, grads, features, out):
    for spot in range(8):
        for k in range(2):
            first = pl.multiple_of(order[spot + 8 * k] * 512, 512)
            out[spot, k] = grads[:, pl.ds(first, 512)]
        out[spot, 2] = features[...]


def pack_tokens(order, grads, features):
    vmem = pl.BlockSpec(memory_space=pltpu.VMEM)
    return pl.pallas_call(
        tokens_kernel,
        out_shape=jax.ShapeDtypeStruct((8, 3, 128, 512), jnp.bfloat16),
        in_specs=[pl.BlockSpec(memory_space=pltpu.SMEM), vmem, vmem],
        out_specs=vmem,
        compiler_params=pltpu.CompilerParams(vmem_limit_bytes=60 * MIB),
    )(order, grads, features)


def slots_kernel(live, rows, owner_col, owner_row, deltas, out):
    count = deltas.shape[0]
    before = lax.broadcasted_iota(jnp.int32, (count, count), 0)
    after = lax.broadcasted_iota(jnp.int32, (count, count), 1)
    same = (owner_col[...] == owner_row[...]) & (before < after)
    rank = jnp.sum(same.astype(jnp.float32), axis=0, keepdims=True)
    position = owner_row[...].astype(jnp.float32) * 16.0 + rank
    place = lax.broadcasted_iota(jnp.int32, (256, count), 0).astype(jnp.float32) == position
    place = place.astype(jnp.float32).astype(jnp.bfloat16)
    masked = jnp.where(before < live[0], deltas[...].astype(jnp.float32), 0.0).astype(jnp.bfloat16)
    high, low = rows[...] // 16, rows[...] % 16
    keys = jnp.where(after < 64, high, low).astype(jnp.float32).astype(jnp.bfloat16)
    moved = jnp.dot(place, masked, preferred_element_type=jnp.float32).astype(jnp.bfloat16)
    named = jnp.dot(place, keys, preferred_element_type=jnp.float32).astype(jnp.bfloat16)
    out[:, 0:16, :] = moved.reshape(16, 16, 128)
    out[:, 16:32, :] = named.reshape(16, 16, 128)


def pack_slots(live, rows, owner, deltas):
    vmem = pl.BlockSpec(memory_space=pltpu.VMEM)
    return pl.pallas_call(
        slots_kernel,
        out_shape=jax.ShapeDtypeStruct((16, 32, 128), jnp.bfloat16),
        in_specs=[pl.BlockSpec(memory_space=pltpu.SMEM), vmem, vmem, vmem, vmem],
        out_specs=vmem,
    )(live, rows.reshape(-1, 1), owner, owner.reshape(1, -1), deltas)


def grad_kernel(half, tokens, out):
    first = pl.multiple_of(half[0] * 128, 128)
    second = pl.multiple_of(256 + half[0] * 128, 128)
    left = jnp.concatenate(
        [
            tokens[:, 2, :, pl.ds(first, 128)].reshape(1024, 128),
            tokens[:, 2, :, pl.ds(second, 128)].reshape(1024, 128),
        ],
        axis=1,
    )
    for k in range(2):
        result = lax.dot_general(
            left,
            tokens[:, k, :, :].reshape(1024, 512),
            (((0,), (0,)), ((), ())),
            preferred_element_type=jnp.float32,
        )
        out[k] = result.reshape(2, 128, 512)


def partial_grads(half, tokens):
    return pl.pallas_call(
        grad_kernel,
        out_shape=jax.ShapeDtypeStruct((2, 2, 128, 512), jnp.float32),
        in_specs=[pl.BlockSpec(memory_space=pltpu.SMEM), pl.BlockSpec(memory_space=pltpu.VMEM)],
        out_specs=pl.BlockSpec(memory_space=pltpu.VMEM),
        compiler_params=pltpu.CompilerParams(vmem_limit_bytes=32 * MIB),
        cost_estimate=pl.CostEstimate(flops=1 << 29, bytes_accessed=4 * MIB, transcendentals=0),
    )(half, tokens)


def encode(tiles):
    largest = jnp.abs(tiles[0])
    for tile in tiles[1:]:
        largest = jnp.maximum(largest, jnp.abs(tile))
    largest = jnp.max(jnp.max(largest, axis=1, keepdims=True), axis=2, keepdims=True)
    grade = jnp.ceil(8.0 * jnp.log2(jnp.maximum(largest, 1e-30))) + 1.0
    factor = CODE_RANGE * jnp.exp2(grade * -0.125)
    words, low = [], None
    for t, tile in enumerate(tiles):
        whole = jnp.round(jnp.clip(tile * factor, -CODE_RANGE, CODE_RANGE)).astype(jnp.int32)
        words.append(whole >> 4)
        nibble = (whole & 15) << (4 * t)
        low = nibble if low is None else low | nibble
    spot = lax.broadcasted_iota(jnp.int32, low.shape, 1) + lax.broadcasted_iota(
        jnp.int32, low.shape, 2
    )
    words.append(jnp.where(spot == 0, grade.astype(jnp.int32), low))
    return jnp.concatenate(words, axis=1).astype(jnp.int16)


def decode(words):
    words = words.astype(jnp.int32)
    low = words[:, 32:40, :]
    grade = low[:, 0:1, 0:1].astype(jnp.float32)
    factor = jnp.exp2(grade * 0.125) * (1.0 / CODE_RANGE)
    tiles = []
    for t in range(4):
        whole = words[:, 8 * t : 8 * t + 8, :] * 16 + ((low >> (4 * t)) & 15)
        tiles.append(whole.astype(jnp.float32) * factor)
    return tiles


def share_kernel(kept, arrived, out):
    tiles = []
    for t in range(4):
        cut = slice(t * 128, (t + 1) * 128)
        tiles.append((kept[:, :, :, cut] + arrived[:, :, :, cut]).reshape(64, 8, 128))
    out[...] = encode(tiles)


def share(kept, arrived):
    vmem = pl.BlockSpec(memory_space=pltpu.VMEM)
    return pl.pallas_call(
        share_kernel,
        out_shape=jax.ShapeDtypeStruct((64, 40, 128), jnp.int16),
        in_specs=[vmem, vmem],
        out_specs=vmem,
        compiler_params=pltpu.CompilerParams(vmem_limit_bytes=32 * MIB),
    )(kept, arrived)


def total_kernel(terms, out):
    words = encode([jnp.sum(tile, axis=0, keepdims=True) for tile in decode(terms[...])])
    out[...] = jnp.broadcast_to(words.astype(jnp.int32), (32, 40, 128)).astype(jnp.int16)


def total(terms):
    vmem = pl.BlockSpec(memory_space=pltpu.VMEM)
    return pl.pallas_call(
        total_kernel,
        out_shape=jax.ShapeDtypeStruct((32, 40, 128), jnp.int16),
        in_specs=[vmem],
        out_specs=vmem,
        compiler_params=pltpu.CompilerParams(vmem_limit_bytes=32 * MIB),
    )(terms)


def parts_of(value):
    high = value.astype(jnp.bfloat16)
    return high, (value - high.astype(jnp.float32)).astype(jnp.bfloat16)


def product(a, b, contract):
    return lax.dot_general(a, b, (contract, ((), ())), preferred_element_type=jnp.float32)


def symmetric_product(high, low, contract):
    side = product(high, low, contract)
    return product(high, high, contract) + (side + jnp.transpose(side))


def rows_product(rows, b):
    bh, bl = b
    count = rows.shape[0]
    high, low = parts_of(rows)
    both = jnp.concatenate([high.astype(jnp.float32), low.astype(jnp.float32)], axis=0)
    first = product(both.astype(jnp.bfloat16), bh, ((1,), (0,)))
    return first[:count] + (first[count:] + product(high, bl, ((1,), (0,))))


def direction_kernel(place, own, other, out, grad, power, square):
    half, first_row = place[0], pl.multiple_of(place[1], 8)
    for side, words in ((half, own), (1 - half, other)):
        for t, tile in enumerate(decode(words[...])):
            tile = tile.reshape(2, 128, 128)
            for k in range(2):
                rows = pl.ds(pl.multiple_of(k * 256 + side * 128, 128), 128)
                grad[rows, t * 128 : (t + 1) * 128] = tile[k]
    g = grad[...]
    width = g.shape[0]
    frobenius = jnp.sum(g * g) + 1e-06
    g_parts = parts_of(g)
    inverse = 1.0 / jnp.sqrt(frobenius)
    normal = symmetric_product(*g_parts, ((1,), (1,))) * inverse * inverse
    n_parts = parts_of(normal)
    squared = symmetric_product(*n_parts, ((1,), (1,)))
    total = jnp.sum(jnp.sum(squared * squared, axis=0, keepdims=True), axis=1, keepdims=True)
    bound = jnp.sqrt(jnp.sqrt(total))
    scale = frobenius * bound
    to_m = 1.0 / bound
    to_m2 = to_m * to_m
    power[...] = normal
    square[...] = squared
    diagonal = lax.broadcasted_iota(jnp.int32, (width, width), 0) == lax.broadcasted_iota(
        jnp.int32, (width, width), 1
    )
    f2 = jnp.where(diagonal, 25.0 / 16.0, 0.0) + (
        normal * (to_m * (-10.0 / 16.0)) + squared * (to_m2 / 16.0)
    )
    f_parts = parts_of(f2)
    m_rows = power[pl.ds(first_row, 8), :] * to_m
    m2_rows = square[pl.ds(first_row, 8), :] * to_m2
    basis = lax.broadcasted_iota(jnp.int32, (8, width), 1) == first_row + lax.broadcasted_iota(
        jnp.int32, (8, width), 0
    )
    f_rows = (jnp.where(basis, 5.0, 0.0) - m_rows) / 4.0
    fm_rows = (5.0 * m_rows - m2_rows) / 4.0
    root = (5.0 * f_rows - rows_product(rows_product(fm_rows, f_parts), f_parts)) / 4.0
    m_root = rows_product(root, n_parts) * to_m
    m2_root = rows_product(m_root, n_parts) * to_m
    f_rows = (5.0 * root - m_root) / 4.0
    fm_rows = (5.0 * m_root - m2_root) / 4.0
    root = (5.0 * f_rows - rows_product(rows_product(fm_rows, f_parts), f_parts)) / 4.0
    quarter = 1.0 / jnp.sqrt(jnp.sqrt(scale))
    result = rows_product(root * quarter, g_parts) * quarter * float(width)
    out[...] = result.astype(jnp.bfloat16)


def direction_rows(place, own, other):
    vmem = pl.BlockSpec(memory_space=pltpu.VMEM)
    square = pltpu.VMEM((512, 512), jnp.float32)
    return pl.pallas_call(
        direction_kernel,
        out_shape=jax.ShapeDtypeStruct((8, 512), jnp.bfloat16),
        in_specs=[pl.BlockSpec(memory_space=pltpu.SMEM), vmem, vmem],
        out_specs=vmem,
        scratch_shapes=[square, square, square],
        compiler_params=pltpu.CompilerParams(vmem_limit_bytes=40 * MIB),
    )(place, own, other)


def update_kernel(got, table, accum, new_table, new_accum):
    deltas = got[:, 0:16, :].reshape(256, 128)
    keys = got[:, 16:32, :].astype(jnp.float32).reshape(256, 128)
    row = keys[:, 0:1] * 16.0 + keys[:, 64:65]
    count = table.shape[0]
    named = row == lax.broadcasted_iota(jnp.int32, (256, count), 1).astype(jnp.float32)
    named = named.astype(jnp.float32).astype(jnp.bfloat16)
    summed = lax.dot_general(
        named, deltas, (((0,), (0,)), ((), ())), preferred_element_type=jnp.float32
    )
    before = jnp.transpose(jnp.broadcast_to(accum[...], (128, count)))
    after = before + jnp.sum(summed * summed, axis=1, keepdims=True) / 128.0
    new_table[...] = table[...] - summed / jnp.sqrt(after)
    new_accum[...] = jnp.transpose(after)[0:1, :]


def update_rows(got, table, accum):
    vmem = pl.BlockSpec(memory_space=pltpu.VMEM)
    return pl.pallas_call(
        update_kernel,
        out_shape=(
            jax.ShapeDtypeStruct(table.shape, jnp.float32),
            jax.ShapeDtypeStruct((1, accum.shape[0]), jnp.float32),
        ),
        in_specs=[vmem, vmem, vmem],
        out_specs=(vmem, vmem),
    )(got, table, accum.reshape(1, -1))


def shards(
    features,
    output_grads,
    block_order,
    emb_table,
    row_accum,
    hot_rows,
    hot_owner,
    live_counts,
    hot_deltas,
):
    group, replica = lax.axis_index("grp"), lax.axis_index("rep")
    core, z = group % 2, group // 2
    x, y = replica // SIDE, replica % SIDE
    exchange = partial(lax.all_to_all, split_axis=0, concat_axis=0, tiled=True)

    slots = pack_slots(live_counts, hot_rows, hot_owner, hot_deltas)

    message = pack_tokens(block_order, output_grads, features)
    tokens = exchange(message, AXES, axis_index_groups=cube_groups())
    tokens, slots = lax.optimization_barrier((tokens, slots))

    away = partial_grads((1 - core).reshape(1), tokens)
    arrived = lax.ppermute(away, AXES, core_pairs())
    kept = partial_grads(core.reshape(1), tokens)
    terms = exchange(share(kept, arrived), AXES, axis_index_groups=stride_groups(False))
    own = exchange(total(terms), AXES, axis_index_groups=stride_groups(True))
    got = exchange(slots, "grp")
    other = lax.ppermute(own, AXES, core_pairs())
    turn = piece(x, y, z)
    first_row = (turn // 16) * 256 + core * 128 + (turn % 16) * 8
    rows = direction_rows(jnp.stack([core, first_row]).astype(jnp.int32), own, other)
    home = lax.ppermute(rows, AXES, home_pairs())

    new_table, new_accum = update_rows(got, emb_table, row_accum)
    home, new_accum = lax.optimization_barrier((home, new_accum))
    directions = exchange(jnp.broadcast_to(home[None], (16, 8, 512)), "grp")
    return (new_table, new_accum.reshape(-1), directions)


def solution(mesh):
    return jax.shard_map(
        shards,
        mesh=mesh,
        in_specs=(
            P(AXES, None),
            P(AXES, None),
            P(),
            P(AXES, None),
            P(AXES),
            P(AXES),
            P(AXES, None),
            P(AXES),
            P(AXES, None),
        ),
        out_specs=(P(AXES, None), P(AXES), P(None, "rep", None)),
        check_vma=False,
    )
```
